256 devices in a mesh: dp: 8 (over y, core), head: 32 (over x, z).
Axes of the slice: x: 4, y: 4, z: 8, core: 2. Of those that a mesh axis runs over, the one named last changes fastest.
Arguments:
- queries: bfloat16 [256, 32, 8192], P(('dp', 'head')), may hold values from -0.59765625 to 0.59765625
- keys: bfloat16 [256, 32, 8192], P(('dp', 'head')), may hold values from -6 to 6
- values: bfloat16 [256, 32, 8192], P(('dp', 'head')), may hold values from -6 to 6
- gate: bfloat16 [256, 32, 8192], P(('dp', 'head')), may hold values from -6 to 6
- states: bfloat16 [256, 64, 128, 128], P('dp', 'head'), may hold values from -6 to 6
- decay: float32 [64], P('head'), may hold values from 0.002 to 0.2
- ancestors: int32 [256, 32, 32], P('dp'), may hold values from 0 to 1, as said below
- tree_sizes: int32 [256], P('dp'), may hold values from 1 to 32, as said below
- gain: float32 [8192], replicated, may hold values from 0.5 to 1.5
- out_weight: bfloat16 [8192, 6144], P(None, 'head'), may hold values from -0.0625 to 0.0625
Outputs:
- projected: bfloat16 [256, 32, 6144], P('dp', None, 'head')
The draws below stay inside these ranges and needn't reach their ends.
Inputs may be any that keep to these rules, and one draw needn't show every extreme that they name: ancestors[r, i, j] is 1 exactly when node j is node i or an ancestor of it; every node but node 0 has a parent of lower index, node 0 is the root. Nodes 0 to tree_sizes[r] - 1 are live; some request has all 32.
All inputs are finite; a program needn't handle non-finite values.
Results may differ from the reference program's by a relative error of at most 0.0062.
Values may be sent and summed in bfloat16 or wider, within the bound.
No kernel may reach another device: no remote copies, remote signals or barrier semaphores. Data moves between devices by JAX's collectives and lax.ppermute only.
A program may use at most 128 MiB of HBM per device.

```python
import math
import jax
import jax.numpy as jnp
from jax import lax

HEADS = 64
HD = 128
DM = 6144
NODES = 32
REQS = 256


def draw_ancestors(key, part):
    key = jax.random.fold_in(key, 11)
    raw = jax.random.randint(key, (REQS, NODES), 0, 1 << 20)
    index = jnp.arange(NODES, dtype=jnp.int32)
    parent = raw % jnp.maximum(index, 1)[None, :]
    parent = jnp.where(index[None, :] == 0, 0, parent)
    links = (parent[:, :, None] == index[None, None, :]).astype(jnp.int32)
    links = jnp.maximum(links, jnp.eye(NODES, dtype=jnp.int32)[None, :, :])
    for turn in range(NODES.bit_length() + 1):
        joined = jnp.einsum('rik,rkj->rij', links, links)
        links = jnp.minimum(joined, 1).astype(jnp.int32)
    return links


def draw_tree_sizes(key, part):
    key = jax.random.fold_in(key, 23)
    first, second = jax.random.split(key)
    sizes = jax.random.randint(first, (REQS,), 1, NODES + 1)
    where = jax.random.randint(second, (), 0, REQS)
    return sizes.at[where].set(NODES).astype(jnp.int32)


def levels(rng, dims, pieces, least, largest):
    loudness = 1.0
    for position, shards_of in pieces:
        steps = jax.random.uniform(jax.random.fold_in(jax.random.fold_in(rng, 6), position), (shards_of,), jnp.float32, least / len(pieces), largest / len(pieces))
        loudness = loudness * jnp.repeat(jnp.exp(steps), dims[position] // shards_of).reshape((-1,) + (1,) * (len(dims) - 1 - position))
    return loudness


def noise(stream_key, dims, width, reach, pieces=(), held_as=jnp.bfloat16):
    loudness = levels(stream_key, dims, pieces, -0.22, 0.18) if pieces else 1.0
    array = jax.random.normal(stream_key, dims, jnp.float32) * width * loudness
    return jnp.minimum(jnp.maximum(array, -reach), reach).astype(held_as)


def setup_inputs(seed: int = 0) -> dict:
    seeds = jax.random.split(jax.random.key(seed), 11)
    return {
        "queries": noise(seeds[0], (REQS, NODES, HEADS * HD), 0.09, 0.59765625, ((0, 256),)),
        "keys": noise(seeds[1], (REQS, NODES, HEADS * HD), 1.0, 6.0, ((0, 256),)),
        "values": noise(seeds[2], (REQS, NODES, HEADS * HD), 1.0, 6.0, ((0, 256),)),
        "gate": noise(seeds[3], (REQS, NODES, HEADS * HD), 1.0, 6.0, ((0, 256),)),
        "states": noise(seeds[4], (REQS, HEADS, HD, HD), 1.0, 6.0, ((0, 8), (1, 32))),
        "decay": jnp.clip(jnp.exp(math.log(0.2) - 4.6051702 * jax.random.uniform(seeds[5], (HEADS,), jnp.float32) ** levels(seeds[5], (HEADS,), ((0, 32),), -0.2, 0.2)), 0.002, 0.2),
        "ancestors": draw_ancestors(jax.random.fold_in(seeds[10], 71), 0),
        "tree_sizes": draw_tree_sizes(jax.random.fold_in(seeds[10], 71), 0),
        "gain": jnp.clip(1.0 + 0.1 * jax.random.normal(seeds[8], (HEADS * HD,), jnp.float32), 0.5, 1.5),
        "out_weight": noise(seeds[9], (HEADS * HD, DM), (HEADS * HD) ** -0.5, 0.0625, ((1, 32),)),
    }


def reference(queries, keys, values, gate, states, decay, ancestors, tree_sizes, gain, out_weight):
    count = queries.shape[0]
    qf = queries.astype(jnp.float32).reshape(count, NODES, HEADS, HD)
    kf = keys.astype(jnp.float32).reshape(count, NODES, HEADS, HD)
    vf = values.astype(jnp.float32).reshape(count, NODES, HEADS, HD)
    anc = ancestors.astype(jnp.float32)
    depth = lax.optimization_barrier(jnp.sum(anc, axis=-1))
    live = (jnp.arange(NODES, dtype=jnp.int32)[None, :] < tree_sizes[:, None]).astype(jnp.float32)
    spread = depth[:, :, None] - depth[:, None, :]
    factor = anc[:, None, :, :] * jnp.exp(-decay[None, :, None, None] * spread[:, None, :, :])
    scores = jnp.einsum('rihd,rjhd->rhij', qf, kf)
    mixed = (scores * factor).astype(jnp.bfloat16)
    mixed = lax.optimization_barrier(mixed).astype(jnp.float32)
    intra = jnp.einsum('rhij,rjhe->rihe', mixed, vf)
    inter = jnp.einsum('rihd,rhde->rihe', qf, states.astype(jnp.float32))
    inter = inter * jnp.exp(-decay[None, None, :, None] * depth[:, :, None, None])
    attn = ((inter + intra) * live[:, :, None, None]).reshape(count, NODES, HEADS * HD).astype(jnp.bfloat16)
    wide = attn.astype(jnp.float32)
    meansq = lax.optimization_barrier(jnp.mean(wide * wide, axis=-1, keepdims=True))
    normed = (wide * lax.rsqrt(meansq + 1e-06) * gain * jax.nn.sigmoid(gate.astype(jnp.float32))).astype(jnp.bfloat16)
    flat = jnp.dot(normed.reshape(count * NODES, HEADS * HD), out_weight, preferred_element_type=jnp.float32)
    return flat.astype(jnp.bfloat16).reshape(count, NODES, DM)
```

```python
import functools
import jax
import jax.numpy as jnp
from jax import lax
from jax.experimental import pallas as pl
from jax.experimental.pallas import tpu as pltpu
from jax.sharding import PartitionSpec as P

NX = 4
NZ = 8
NODES = 32
HD = 128
PAIR = 2 * HD
QUART = 2048
COLS = 192
ROWS = NX * NODES
WIDE = QUART + 128
ZSHIFTS = (1, 7, 2, 6, 3, 5, 4)
NT = (((1,), (1,)), ((), ()))
BF = jnp.bfloat16
F32 = jnp.float32


def zsend(array, shift):
    pairs = [(x * NZ + z, x * NZ + (z + shift) % NZ) for x in range(NX) for z in range(NZ)]
    return lax.ppermute(array, "head", pairs)


def xsend(array, shift):
    pairs = [(x * NZ + z, ((x + shift) % NX) * NZ + z) for x in range(NX) for z in range(NZ)]
    return lax.ppermute(array, "head", pairs)


def split3(value):
    hi = lax.reduce_precision(value, 8, 7)
    mid = lax.reduce_precision(value - hi, 8, 7)
    return hi, mid, value - hi - mid


def attend_kernel(pos, sizes, x0, x1, x2, x3, anc_ref, msg_ref, gain_ref, u_ref, ss_ref):
    x, z = pos[0], pos[1]
    extra = msg_ref[NX * PAIR : NX * PAIR + 16, :].astype(F32)
    rates = [extra[3 * j : 3 * j + 1] + extra[3 * j + 1 : 3 * j + 2] + extra[3 * j + 2 : 3 * j + 3] for j in range(2)]
    node = lax.broadcasted_iota(jnp.int32, (NODES, HD), 0)
    for slot, part in enumerate((x0, x1, x2, x3)):
        xa = lax.rem(x - slot + NX, NX)
        row = pl.multiple_of(xa * NODES, NODES)
        anc = anc_ref[xa, 0].astype(F32)
        depth = jnp.sum(anc, axis=1, keepdims=True)
        depth_t = lax.dot_general(jnp.ones((8, NODES), BF), anc.astype(BF), NT, preferred_element_type=F32)[0:1]
        live = (node < sizes[xa * NZ + z]).astype(F32)
        total = jnp.zeros((NODES, 1), F32)
        for j in range(2):
            cols = slice(j * HD, (j + 1) * HD)
            q = part[0, :, cols]
            k = part[1, :, cols]
            v = part[2, :, cols]
            state = msg_ref[pl.ds(pl.multiple_of((xa * 2 + j) * HD, HD), HD), :]
            rate = rates[j]
            scores = lax.dot_general(q, k, NT, preferred_element_type=F32)
            factor = anc * jnp.exp(-rate[:, :NODES] * (depth - depth_t))
            mix = (scores * factor).astype(BF)
            intra = jnp.dot(mix, v, preferred_element_type=F32)
            inter = jnp.dot(q, state, preferred_element_type=F32)
            attn = (live * (inter * jnp.exp(-rate * depth) + intra)).astype(BF).astype(F32)
            total = total + jnp.sum(attn * attn, axis=1, keepdims=True)
            scale = gain_ref[:, cols] / (1.0 + jnp.exp(-part[3, :, cols].astype(F32)))
            u_ref[pl.ds(row, NODES), cols] = (attn * scale).astype(BF)
        ss_ref[pl.ds(row, NODES), :] = jnp.broadcast_to(total, (NODES, 128))


def attend(pos, sizes, parts, anc, msg, gain):
    part_spec = pl.BlockSpec((4, NODES, PAIR), lambda i, pos, sizes: (0, 0, pos[2]))
    return pl.pallas_call(
        attend_kernel,
        grid_spec=pltpu.PrefetchScalarGridSpec(
            num_scalar_prefetch=2,
            grid=(1,),
            in_specs=[part_spec] * 4
            + [
                pl.BlockSpec((NX, 1, NODES, NODES), lambda i, pos, sizes: (0, pos[1], 0, 0)),
                pl.BlockSpec((NX * PAIR + 16, HD), lambda i, pos, sizes: (0, 0)),
                pl.BlockSpec((1, PAIR), lambda i, pos, sizes: (0, pos[0] * NZ + pos[2])),
            ],
            out_specs=[
                pl.BlockSpec((ROWS, PAIR), lambda i, pos, sizes: (0, 0)),
                pl.BlockSpec((ROWS, 128), lambda i, pos, sizes: (0, 0)),
            ],
        ),
        out_shape=[
            jax.ShapeDtypeStruct((ROWS, PAIR), BF),
            jax.ShapeDtypeStruct((ROWS, 128), F32),
        ],
        cost_estimate=pl.CostEstimate(flops=100_000_000, bytes_accessed=1_000_000, transcendentals=100_000),
    )(pos, sizes, *parts, anc, msg, gain)


def gather_kernel(pos, *refs):
    us, sums, out = refs[:NZ], refs[NZ : 2 * NZ], refs[2 * NZ]
    z = pos[1]
    total = sums[0][...]
    for ref in sums[1:]:
        total = total + ref[...]
    for shift, ref in zip((0,) + ZSHIFTS, us):
        col = lax.rem(z - shift + NZ, NZ) * PAIR
        out[:, pl.ds(pl.multiple_of(col, PAIR), PAIR)] = ref[...]
    hi = total.astype(BF).astype(F32)
    mid = (total - hi).astype(BF).astype(F32)
    low = total - hi - mid
    lane = lax.broadcasted_iota(jnp.int32, (ROWS, 128), 1)
    tail = jnp.where(lane == 64, hi, jnp.where(lane == 65, mid, jnp.where(lane == 66, low, 0.0)))
    out[:, QUART:WIDE] = tail.astype(BF)


def assemble(pos, us, sums):
    return pl.pallas_call(
        gather_kernel,
        in_specs=[pl.BlockSpec(memory_space=pltpu.SMEM)] + [pl.BlockSpec(memory_space=pltpu.VMEM)] * (2 * NZ),
        out_specs=pl.BlockSpec(memory_space=pltpu.VMEM),
        out_shape=jax.ShapeDtypeStruct((ROWS, WIDE), BF),
        cost_estimate=pl.CostEstimate(flops=1_000_000, bytes_accessed=2_000_000, transcendentals=0),
    )(pos, *us, *sums)


def project_kernel(count, *refs):
    pieces, weights, outs = refs[:count], refs[count : count + NX], refs[count + NX :]
    row = 0
    for piece in pieces:
        size = piece.shape[0]
        rows = slice(row, row + size)
        u = piece[:, :QUART]
        tail = piece[:, QUART + 64 : WIDE]
        for weight, out in zip(weights, outs):
            acc = lax.dot_general(u, weight[...], NT, preferred_element_type=F32)
            out[rows, :COLS] = acc.astype(out.dtype)
            out[rows, COLS:] = tail.astype(out.dtype)
        row += size


def project(pieces, weights):
    rows = sum(p.shape[0] for p in pieces)
    flops = 2 * rows * QUART * COLS * NX
    return pl.pallas_call(
        functools.partial(project_kernel, len(pieces)),
        in_specs=[pl.BlockSpec(memory_space=pltpu.VMEM)] * (len(pieces) + NX),
        out_specs=[pl.BlockSpec(memory_space=pltpu.VMEM)] * NX,
        out_shape=[jax.ShapeDtypeStruct((rows, 256), F32)] + [jax.ShapeDtypeStruct((rows, 256), BF)] * (NX - 1),
        cost_estimate=pl.CostEstimate(flops=flops, bytes_accessed=4_000_000, transcendentals=0),
        compiler_params=pltpu.CompilerParams(vmem_limit_bytes=32 * 1024 * 1024),
    )(*pieces, *weights)


def finish_kernel(layout, pos, *refs):
    out = refs[-1]
    z = pos[1]
    for g, places in enumerate(layout):
        own, a, b, c = refs[4 * g : 4 * g + 4]
        row = 0
        for shift, first, last in places:
            size = (last - first) * NODES
            rows = slice(row, row + size)
            total = own[rows, :] + a[rows, :].astype(F32) + b[rows, :].astype(F32) + c[rows, :].astype(F32)
            squares = total[:, COLS : COLS + 1] + total[:, COLS + 1 : COLS + 2] + total[:, COLS + 2 : COLS + 3]
            scaled = total[:, :COLS] * lax.rsqrt(squares * (1.0 / 8192.0) + 1e-06)
            source = lax.rem(z - shift + 2 * NZ, NZ)
            for x in range(first, last):
                part = scaled[(x - first) * NODES : (x - first + 1) * NODES]
                out[x, source] = part.astype(BF)
            row += size


def finish(pos, groups, layout):
    flat = [a for group in groups for a in group]
    return pl.pallas_call(
        functools.partial(finish_kernel, layout),
        in_specs=[pl.BlockSpec(memory_space=pltpu.SMEM)] + [pl.BlockSpec(memory_space=pltpu.VMEM)] * len(flat),
        out_specs=pl.BlockSpec(memory_space=pltpu.VMEM),
        out_shape=jax.ShapeDtypeStruct((NX, NZ, NODES, COLS), BF),
        cost_estimate=pl.CostEstimate(flops=2_000_000, bytes_accessed=4_000_000, transcendentals=0),
        compiler_params=pltpu.CompilerParams(vmem_limit_bytes=32 * 1024 * 1024),
    )(pos, *flat)


def per_device(queries, keys, values, gate, states, decay, ancestors, tree_sizes, gain, out_weight):
    me = lax.axis_index("head")
    x, z = me // NZ, me % NZ

    four = jnp.stack([queries[0], keys[0], values[0], gate[0]])

    def quarter(shift):
        return lax.dynamic_slice_in_dim(four, ((x + shift) % NX) * QUART, QUART, axis=2)

    parts = [quarter(0)] + [xsend(quarter(d), d) for d in range(1, NX)]

    hi, mid, low = split3(decay)
    rows = jnp.stack([hi[0], mid[0], low[0], hi[1], mid[1], low[1]])
    rows = jnp.concatenate([rows, jnp.zeros((10,), F32)]).astype(BF)
    extra = jnp.broadcast_to(rows[:, None], (16, HD))
    by_z = states.reshape(NX, NZ, 2, HD, HD)

    def message(shift):
        block = lax.dynamic_index_in_dim(by_z, (z + shift) % NZ, axis=1, keepdims=False)
        return jnp.concatenate([block.reshape(NX * PAIR, HD), extra])

    messages = [message(0)] + [zsend(message(d), d) for d in ZSHIFTS]

    weight = out_weight.T
    def weight_quarter(shift):
        return lax.dynamic_slice_in_dim(weight, ((x + shift) % NX) * QUART, QUART, axis=1)

    weights = [weight_quarter(0)] + [xsend(weight_quarter(d), d) for d in range(1, NX)]

    anc = ancestors.reshape(NX, NZ, NODES, NODES)
    gain = gain.reshape(1, -1)
    us, sums = [], []
    for shift, msg in zip((0,) + ZSHIFTS, messages):
        pos = jnp.stack([x, z, (z - shift) % NZ]).astype(jnp.int32)
        u, ss = attend(pos, tree_sizes, parts, anc, msg, gain)
        us.append(u)
        sums.append(ss)
    here = jnp.stack([x, z]).astype(jnp.int32)
    own = assemble(here, us, sums)

    up = dn = own
    batches = [[own]]
    layout = [[(0, 0, NX)]]
    for step in range(1, 4):
        up, dn = zsend(up, 1), zsend(dn, -1)
        batches.append([up, dn])
        layout.append([(step, 0, NX), (-step, 0, NX)])
    half = ROWS // 2
    batches.append([zsend(up[:half], 1), zsend(dn[half:], -1)])
    layout.append([(4, 0, NX // 2), (-4, NX // 2, NX)])
    batches[1] = batches[0] + batches[1]
    layout[1] = layout[0] + layout[1]

    groups = []
    for pieces in batches[1:]:
        own_part, *others = project(pieces, weights)
        groups.append([own_part] + [xsend(p, -d) for d, p in enumerate(others, 1)])
    out = finish(here, groups, layout[1:])
    return out.reshape(NX * NZ, NODES, COLS)


def solution(mesh):
    return jax.shard_map(
        per_device,
        mesh=mesh,
        in_specs=(
            P(("dp", "head"), None, None),
            P(("dp", "head"), None, None),
            P(("dp", "head"), None, None),
            P(("dp", "head"), None, None),
            P("dp", "head", None, None),
            P("head"),
            P("dp", None, None),
            P("dp"),
            P(),
            P(None, "head"),
        ),
        out_specs=P("dp", None, "head"),
        check_vma=False,
    )
```

```python
import functools
import jax
import jax.numpy as jnp
from jax import lax
from jax.experimental import pallas as pl
from jax.experimental.pallas import tpu as pltpu
from jax.sharding import PartitionSpec as P

NX = 4
NZ = 8
NODES = 32
HEADS = 64
HD = 128
PAIR = 2 * HD
QUART = 2048
HALF = QUART // 2
COLS = 192
ROWS = NX * NODES
QROWS = 2 * NODES + 16
NT = (((1,), (1,)), ((), ()))
BF = jnp.bfloat16
F32 = jnp.float32
ANY = pl.BlockSpec(memory_space=pl.ANY)
HBM = pl.BlockSpec(memory_space=pltpu.HBM)
VMEM = pl.BlockSpec(memory_space=pltpu.VMEM)
SMEM = pl.BlockSpec(memory_space=pltpu.SMEM)
PARAMS = pltpu.CompilerParams(vmem_limit_bytes=16 * 1024 * 1024)


def zsend(array, shift):
    pairs = [(x * NZ + z, x * NZ + (z + shift) % NZ) for x in range(NX) for z in range(NZ)]
    return lax.ppermute(array, "head", pairs)


def xsend(array, shift):
    pairs = [(x * NZ + z, ((x + shift) % NX) * NZ + z) for x in range(NX) for z in range(NZ)]
    return lax.ppermute(array, "head", pairs)


def swap_core(array):
    return lax.ppermute(array, "dp", [(i, i ^ 1) for i in range(8)])


def place():
    me = lax.axis_index("head")
    return lax.div(me, NZ), lax.rem(me, NZ)


def core():
    return lax.rem(lax.axis_index("dp"), 2)


def cost(flops, size, trans=0):
    return pl.CostEstimate(flops=flops, bytes_accessed=size, transcendentals=trans)


def run_copies(pairs, sems):
    copies = [pltpu.make_async_copy(a, b, sems.at[n]) for n, (a, b) in enumerate(pairs)]
    for copy in copies:
        copy.start()
    return copies


def split3(value):
    hi = value.astype(BF).astype(F32)
    mid = (value - hi).astype(BF).astype(F32)
    return hi, mid, value - hi - mid


def pack_queries_kernel(decay, q_hbm, out, q, sems):
    cuts = [slice(n * QUART, (n + 1) * QUART) for n in range(NX)]
    copies = run_copies([(q_hbm.at[0, :, cut], q.at[:, cut]) for cut in cuts], sems)
    row = lax.broadcasted_iota(jnp.int32, (16, HD), 0)
    rows = jnp.zeros((16, HD), F32)
    for j in range(2):
        for n, piece in enumerate(split3(jnp.full((16, HD), decay[j], F32))):
            rows = jnp.where(row == 3 * j + n, piece, rows)
    tail = rows.astype(BF)
    for n in range(NX * NZ):
        out[n, 2 * NODES :, :] = tail
    for n in range(NX * NZ):
        if n % NZ == 0:
            copies[n // NZ].wait()
        for j in range(2):
            out[n, j * NODES : (j + 1) * NODES, :] = q[:, (2 * n + j) * HD : (2 * n + j + 1) * HD]


def pack_queries(decay, q):
    return pl.pallas_call(
        pack_queries_kernel,
        in_specs=[SMEM, HBM],
        out_specs=VMEM,
        out_shape=jax.ShapeDtypeStruct((NX * NZ, QROWS, HD), BF),
        scratch_shapes=[pltpu.VMEM((NODES, HEADS * HD), BF), pltpu.SemaphoreType.DMA((NX,))],
        cost_estimate=cost(0, 1_000_000),
        compiler_params=pltpu.CompilerParams(vmem_limit_bytes=60 * 1024 * 1024),
    )(decay, q)


def pack_weights_kernel(w, *refs):
    o0, o1, o2, o3, sems = refs[-5:]
    x, _ = place()
    pairs = [(w.at[:, pl.ds(pl.multiple_of(x * QUART, QUART), QUART)], o0)]
    for n, out in enumerate((o1, o2, o3), 1):
        col = pl.multiple_of(lax.rem(x + n, NX) * QUART + core() * HALF, HALF)
        pairs.append((w.at[:, pl.ds(col, HALF)], out))
    for copy in run_copies(pairs, sems):
        copy.wait()


def pack_weights(w, after):
    return pl.pallas_call(
        pack_weights_kernel,
        in_specs=[HBM] + [ANY] * len(after),
        out_specs=[VMEM] * NX,
        out_shape=[jax.ShapeDtypeStruct((COLS, QUART), BF)] + [jax.ShapeDtypeStruct((COLS, HALF), BF)] * 3,
        scratch_shapes=[pltpu.SemaphoreType.DMA((4,))],
        cost_estimate=cost(0, 4_000_000),
        compiler_params=PARAMS,
    )(w, *after)


def inter_kernel(decay, queries, states, anc_ref, *refs):
    out = refs[-1]
    for r in range(NX * NZ):
        depth = jnp.sum(anc_ref[r].astype(F32), axis=1, keepdims=True)
        for j in range(2):
            rows = slice(j * NODES, (j + 1) * NODES)
            inter = jnp.dot(queries[r, rows, :], states[r, j], preferred_element_type=F32)
            value = inter * jnp.exp(jnp.broadcast_to(-decay[j] * depth, (NODES, HD)))
            out[r, :, j * HD : (j + 1) * HD] = value.astype(BF)


def inter_part(decay, queries, states, anc, marks):
    return pl.pallas_call(
        inter_kernel,
        in_specs=[SMEM] + [VMEM] * 3 + [ANY] * len(marks),
        out_specs=VMEM,
        out_shape=jax.ShapeDtypeStruct((NX * NZ, NODES, PAIR), BF),
        cost_estimate=cost(70_000_000, 4_000_000, 100_000),
        compiler_params=PARAMS,
    )(decay, queries, states, anc, *marks)


def intra_kernel(q_ref, k_ref, v_ref, gate_ref, spread_ref, anc_ref, gain_ref, intra_ref, scale_ref):
    anc = anc_ref[lax.axis_index("head")].astype(F32)
    depth = jnp.sum(anc, axis=1, keepdims=True)
    depth_t = lax.dot_general(jnp.ones((8, NODES), BF), anc.astype(BF), NT, preferred_element_type=F32)[0:1]
    gaps = depth - depth_t
    for n in range(NX * NZ):
        extra = spread_ref[n, 2 * NODES :, :].astype(F32)
        for j in range(2):
            cols = slice((2 * n + j) * HD, (2 * n + j + 1) * HD)
            rate = extra[3 * j : 3 * j + 1] + extra[3 * j + 1 : 3 * j + 2] + extra[3 * j + 2 : 3 * j + 3]
            scores = lax.dot_general(q_ref[0, :, cols], k_ref[0, :, cols], NT, preferred_element_type=F32)
            mix = (scores * (anc * jnp.exp(-rate[:, :NODES] * gaps))).astype(BF)
            intra_ref[:, cols] = jnp.dot(mix, v_ref[0, :, cols], preferred_element_type=F32)
            scale_ref[:, cols] = gain_ref[:, cols] / (1.0 + jnp.exp(-gate_ref[0, :, cols].astype(F32)))


def intra_part(q, k, v, gate, spread, anc, gain):
    return pl.pallas_call(
        intra_kernel,
        in_specs=[VMEM] * 7,
        out_specs=[VMEM] * 2,
        out_shape=[jax.ShapeDtypeStruct((NODES, HEADS * HD), F32)] * 2,
        cost_estimate=cost(100_000_000, 4_000_000, 200_000),
        compiler_params=PARAMS,
    )(q, k, v, gate, spread, anc, gain)


def merge_kernel(sizes, inter_ref, intra_ref, scale_ref, o0, o1, o2, o3, attn_ref):
    x, _ = place()
    node = lax.broadcasted_iota(jnp.int32, (NODES, HD), 0)
    live = (node < sizes[lax.axis_index("head")]).astype(F32)
    squares = jnp.zeros((NODES, HD), F32)
    for h in range(HEADS):
        cols = slice(h * HD, (h + 1) * HD)
        inter = inter_ref[h // 2, :, (h % 2) * HD : (h % 2 + 1) * HD].astype(F32)
        attn = (live * (inter + intra_ref[:, cols])).astype(BF)
        attn_ref[:, cols] = attn
        attn = attn.astype(F32)
        squares = squares + attn * attn
    mean = jnp.sum(squares, axis=1, keepdims=True) * (1.0 / (HEADS * HD))
    norm = jnp.broadcast_to(lax.rsqrt(mean + 1e-06), (NODES, HD))
    for shift, out in enumerate((o0, o1, o2, o3)):
        base = lax.rem(x + shift, NX) * QUART
        for h in range(HEADS // NX):
            cols = pl.ds(pl.multiple_of(base + h * HD, HD), HD)
            normed = attn_ref[:, cols].astype(F32) * norm * scale_ref[:, cols]
            out[:, h * HD : (h + 1) * HD] = normed.astype(BF)


def merge(sizes, inter, intra, scale):
    return pl.pallas_call(
        merge_kernel,
        in_specs=[SMEM] + [VMEM] * 3,
        out_specs=[VMEM] * NX,
        out_shape=[jax.ShapeDtypeStruct((NODES, QUART), BF)] * NX,
        scratch_shapes=[pltpu.VMEM((NODES, HEADS * HD), BF)],
        cost_estimate=cost(10_000_000, 4_000_000),
        compiler_params=PARAMS,
    )(sizes, inter, intra, scale)


def stack_kernel(p0, p1, p2, p3, out):
    x, _ = place()
    for slot, part in enumerate((p0, p1, p2, p3)):
        row = pl.multiple_of(lax.rem(x - slot + NX, NX) * NODES, NODES)
        out[pl.ds(row, NODES), :] = part[...]


def stack_rows(parts):
    return pl.pallas_call(
        stack_kernel,
        in_specs=[VMEM] * NX,
        out_specs=VMEM,
        out_shape=jax.ShapeDtypeStruct((ROWS, QUART), BF),
        cost_estimate=cost(0, 1_000_000),
        compiler_params=PARAMS,
    )(*parts)


def project_kernel(count, *refs):
    pieces, (w0, w1, w2, w3, swapped) = refs[:count], refs[count : count + 5]
    outs, lhs = refs[count + 5 : count + 5 + NX], refs[-1]
    mine = pl.multiple_of(core() * HALF, HALF)
    other = pl.multiple_of(HALF - core() * HALF, HALF)
    if count == 1:
        lhs = pieces[0]
    else:
        row = 0
        for piece in pieces:
            lhs[row : row + piece.shape[0], :] = piece[...]
            row += piece.shape[0]
    for n, (weight, out) in enumerate(zip((w0, w1, w2, w3), outs)):
        if n == 0:
            acc = lax.dot_general(lhs[...], weight[...], NT, preferred_element_type=F32)
        else:
            acc = lax.dot_general(lhs[:, pl.ds(mine, HALF)], weight[...], NT, preferred_element_type=F32)
            acc = acc + lax.dot_general(lhs[:, pl.ds(other, HALF)], swapped[n - 1], NT, preferred_element_type=F32)
        out[...] = acc.astype(out.dtype)


def project(pieces, weights):
    rows = sum(p.shape[0] for p in pieces)
    return pl.pallas_call(
        functools.partial(project_kernel, len(pieces)),
        in_specs=[VMEM] * (len(pieces) + 5),
        out_specs=[VMEM] * NX,
        out_shape=[jax.ShapeDtypeStruct((rows, COLS), F32)] + [jax.ShapeDtypeStruct((rows, COLS), BF)] * (NX - 1),
        scratch_shapes=[pltpu.VMEM((rows, QUART), BF)],
        cost_estimate=cost(2 * rows * QUART * COLS * NX, 4_000_000),
        compiler_params=PARAMS,
    )(*pieces, *weights)


def finish_kernel(layout, *refs):
    out = refs[-1]
    _, z = place()
    for g, places in enumerate(layout):
        own, a, b, c = refs[4 * g : 4 * g + 4]
        row = 0
        for shift, first, last in places:
            size = (last - first) * NODES
            rows = slice(row, row + size)
            total = own[rows, :] + a[rows, :].astype(F32) + b[rows, :].astype(F32) + c[rows, :].astype(F32)
            source = lax.rem(z - shift + 2 * NZ, NZ)
            for x in range(first, last):
                part = total[(x - first) * NODES : (x - first + 1) * NODES]
                out[x, source] = part.astype(BF)
            row += size


def finish(groups, layout):
    flat = [a for group in groups for a in group]
    return pl.pallas_call(
        functools.partial(finish_kernel, layout),
        in_specs=[VMEM] * len(flat),
        out_specs=VMEM,
        out_shape=jax.ShapeDtypeStruct((NX, NZ, NODES, COLS), BF),
        cost_estimate=cost(2_000_000, 4_000_000),
        compiler_params=PARAMS,
    )(*flat)


def tie(arrays, *marks):
    return lax.optimization_barrier((*arrays, *marks))[: len(arrays)]


def per_device(queries, keys, values, gate, states, decay, ancestors, tree_sizes, gain, out_weight):
    packed = pack_queries(decay, queries)
    w0, w1, w2, w3 = pack_weights(out_weight.T, [packed])
    w1, w3 = xsend(w1, 1), xsend(w3, 3)
    spread = lax.all_to_all(packed, "head", 0, 0, tiled=True)
    inter = inter_part(decay, spread, states, ancestors, [w1, w3])
    w2 = xsend(tie((w2,), inter)[0], 2)
    inter = lax.all_to_all(inter, "head", 0, 0, tiled=True)
    intra, scale = intra_part(queries, keys, values, gate, spread, ancestors, gain.reshape(1, -1))
    swapped = swap_core(jnp.stack(tie((w1, w2, w3), scale)))
    weights = [w0, w1, w2, w3, swapped]
    n0, n1, n2, n3 = merge(tree_sizes, inter, intra, scale)
    own = stack_rows([n0, xsend(n1, 1), xsend(n2, 2), xsend(n3, 3)])

    groups, layout = [], []
    half = ROWS // 2

    def send_sums(pieces, places):
        own_part, *others = project(pieces, weights)
        groups.append([own_part] + [xsend(p, -d) for d, p in enumerate(others, 1)])
        layout.append(places)
        return own_part

    up, dn = zsend(own, 1), zsend(own, -1)
    mark = send_sums([own], [(0, 0, NX)])
    for step in range(1, 4):
        up, dn = tie((up, dn), *groups[-1])
        pieces = up, dn
        if step < 3:
            up, dn = zsend(up, 1), zsend(dn, -1)
        else:
            up, dn = zsend(up[:half], 1), zsend(dn[half:], -1)
        mark = send_sums(pieces, [(step, 0, NX), (-step, 0, NX)])
    last = tie((up, dn), mark)
    send_sums(last, [(4, 0, NX // 2), (-4, NX // 2, NX)])
    out = finish(groups, layout)
    return out.reshape(NX * NZ, NODES, COLS)


def solution(mesh):
    return jax.shard_map(
        per_device,
        mesh=mesh,
        in_specs=(
            P(("dp", "head"), None, None),
            P(("dp", "head"), None, None),
            P(("dp", "head"), None, None),
            P(("dp", "head"), None, None),
            P("dp", "head", None, None),
            P("head"),
            P("dp", None, None),
            P("dp"),
            P(),
            P(None, "head"),
        ),
        out_specs=P("dp", None, "head"),
        check_vma=False,
    )
```

```python
import functools
import jax
import jax.numpy as jnp
from jax import lax
from jax.experimental import pallas as pl
from jax.experimental.pallas import tpu as pltpu
from jax.sharding import PartitionSpec as P

NX = 4
NZ = 8
NODES = 32
HEADS = 64
HD = 128
PAIR = 2 * HD
QUART = 2048
PART = QUART // 4

NY = 4
COLS = 192
MSG = NODES * 8 + 2 * COLS
HROWS = 64
PIECE = 16 * HROWS + 16
ROWS = NX * NODES
QROWS = 2 * NODES + 16
NT = (((1,), (1,)), ((), ()))
BF = jnp.bfloat16
F32 = jnp.float32
ANY = pl.BlockSpec(memory_space=pl.ANY)
HBM = pl.BlockSpec(memory_space=pltpu.HBM)
VMEM = pl.BlockSpec(memory_space=pltpu.VMEM)
SMEM = pl.BlockSpec(memory_space=pltpu.SMEM)
WIDEST = pltpu.CompilerParams(vmem_limit_bytes=60 * 1024 * 1024)
PARAMS = pltpu.CompilerParams(vmem_limit_bytes=16 * 1024 * 1024)


def zsend(array, shift):
    pairs = [(x * NZ + z, x * NZ + (z + shift) % NZ) for x in range(NX) for z in range(NZ)]
    return lax.ppermute(array, "head", pairs)


def xsend(array, shift):
    pairs = [(x * NZ + z, ((x + shift) % NX) * NZ + z) for x in range(NX) for z in range(NZ)]
    return lax.ppermute(array, "head", pairs)


def swap_y(array):
    return lax.ppermute(array, "dp", [(i, i ^ 2) for i in range(2 * NY)])


def swap_core(array):
    return lax.ppermute(array, "dp", [(i, i ^ 1) for i in range(2 * NY)])


def place():
    me = lax.axis_index("head")
    return lax.div(me, NZ), lax.rem(me, NZ)


def cost(flops, size, trans=0):
    return pl.CostEstimate(flops=flops, bytes_accessed=size, transcendentals=trans)


def run_copies(pairs, sems):
    copies = [pltpu.make_async_copy(a, b, sems.at[n]) for n, (a, b) in enumerate(pairs)]
    for copy in copies:
        copy.start()
    return copies


def split3(value):
    hi = value.astype(BF).astype(F32)
    mid = (value - hi).astype(BF).astype(F32)
    return hi, mid, value - hi - mid


def pack_queries_kernel(decay, q_hbm, out, q, sems):
    cuts = [slice(n * QUART, (n + 1) * QUART) for n in range(NX)]
    copies = run_copies([(q_hbm.at[0, :, cut], q.at[:, cut]) for cut in cuts], sems)
    row = lax.broadcasted_iota(jnp.int32, (16, HD), 0)
    rows = jnp.zeros((16, HD), F32)
    for j in range(2):
        for n, piece in enumerate(split3(jnp.full((16, HD), decay[j], F32))):
            rows = jnp.where(row == 3 * j + n, piece, rows)
    tail = rows.astype(BF)
    for n in range(NX * NZ):
        out[n, 2 * NODES :, :] = tail
    for n in range(NX * NZ):
        if n % NZ == 0:
            copies[n // NZ].wait()
        for j in range(2):
            out[n, j * NODES : (j + 1) * NODES, :] = q[:, (2 * n + j) * HD : (2 * n + j + 1) * HD]


def pack_queries(decay, q):
    return pl.pallas_call(
        pack_queries_kernel,
        in_specs=[SMEM, HBM],
        out_specs=VMEM,
        out_shape=jax.ShapeDtypeStruct((NX * NZ, QROWS, HD), BF),
        scratch_shapes=[pltpu.VMEM((NODES, HEADS * HD), BF), pltpu.SemaphoreType.DMA((NX,))],
        cost_estimate=cost(0, 1_000_000),
        compiler_params=WIDEST,
    )(decay, q)


def pack_messages_kernel(gate_hbm, w, after, w0_hbm, *refs):
    outs_hbm, (gate, w0, outs, sems) = refs[:NX], refs[NX:]
    x, _ = place()
    cuts = [slice(n * QUART, (n + 1) * QUART) for n in range(NX)]
    pairs = [(gate_hbm.at[0, :, cut], gate.at[:, cut]) for cut in cuts]
    bases = [lax.rem(x + n, NX) * QUART for n in range(NX)]
    for n in (2, 1, 3):
        for b in range(2):
            col = pl.multiple_of(bases[n] + lax.rem(lax.axis_index("dp"), 4) * PART + b * PAIR, PAIR)
            pairs.append((w.at[:, pl.ds(col, PAIR)], outs.at[n, pl.ds(NZ * NODES + b * COLS, COLS)]))
    pairs.append((w.at[:, pl.ds(pl.multiple_of(x * QUART, QUART), QUART)], w0))
    copies = run_copies(pairs, sems)
    for copy in copies[:NX]:
        copy.wait()
    sends = []
    for i, n in enumerate((2, 1, 3, 0)):
        for b in range(NZ):
            cols = pl.ds(pl.multiple_of(bases[n] + b * PAIR, PAIR), PAIR)
            outs[n, b * NODES : (b + 1) * NODES, :] = gate[:, cols]
        rows = pl.ds(0, NZ * NODES)
        if n:
            copies[NX + 2 * i].wait()
            copies[NX + 2 * i + 1].wait()
            rows = pl.ds(0, MSG)
        sends.append(pltpu.make_async_copy(outs.at[n, rows], outs_hbm[n].at[rows], sems.at[len(pairs) + n]))
        sends[-1].start()
    copies[-1].wait()
    sends.append(pltpu.make_async_copy(w0, w0_hbm, sems.at[len(pairs) + NX]))
    sends[-1].start()
    for send in sends:
        send.wait()


def pack_messages(gate, w, after):
    return pl.pallas_call(
        pack_messages_kernel,
        in_specs=[HBM] * 2 + [ANY],
        out_specs=[HBM] * (1 + NX),
        out_shape=[jax.ShapeDtypeStruct((COLS, QUART), BF)] + [jax.ShapeDtypeStruct((NZ * NODES, PAIR), BF)]
        + [jax.ShapeDtypeStruct((MSG, PAIR), BF)] * (NX - 1),
        scratch_shapes=[
            pltpu.VMEM((NODES, HEADS * HD), BF),
            pltpu.VMEM((COLS, QUART), BF),
            pltpu.VMEM((NX, MSG, PAIR), BF),
            pltpu.SemaphoreType.DMA((NX + 7 + NX + 1,)),
        ],
        cost_estimate=cost(0, 4_000_000),
        compiler_params=WIDEST,
    )(gate, w, after)


def join_weights_kernel(w0, m0, m1, theirs, out):
    part = lax.rem(lax.axis_index("dp"), 4)
    flip = 1 - 2 * lax.rem(part, 2)
    far = lax.rem(part + 2, 4)
    out[0] = w0[...]
    for s, (ref, mine) in enumerate(((m0, part), (m1, far))):
        for d in range(NX - 1):
            for b in range(2):
                near = pl.ds(pl.multiple_of(mine * PART + b * PAIR, PAIR), PAIR)
                other = pl.ds(pl.multiple_of((mine + flip) * PART + b * PAIR, PAIR), PAIR)
                out[d + 1, :, near] = ref[d, b * COLS : (b + 1) * COLS]
                out[d + 1, :, other] = theirs[s, d, b * COLS : (b + 1) * COLS]


def join_weights(w0, m0, m1, theirs):
    return pl.pallas_call(
        join_weights_kernel,
        in_specs=[VMEM] * 4,
        out_specs=VMEM,
        out_shape=jax.ShapeDtypeStruct((NX, COLS, QUART), BF),
        cost_estimate=cost(0, 6_000_000),
        compiler_params=PARAMS,
    )(w0, m0, m1, theirs)


def inter_kernel(queries, states, *refs):
    out, extras = refs[-2:]
    for r in range(NX * NZ):
        x, z = divmod(r, NZ)
        for j in range(2):
            rows = slice(j * NODES, (j + 1) * NODES)
            inter = jnp.dot(queries[r, rows, :], states[r, j], preferred_element_type=F32)
            out[z, x * NODES : (x + 1) * NODES, j * HD : (j + 1) * HD] = inter.astype(BF)
        extras[r] = queries[r, 2 * NODES :, :]


def inter_part(queries, states, marks):
    return pl.pallas_call(
        inter_kernel,
        in_specs=[VMEM] * 2 + [ANY] * len(marks),
        out_specs=[VMEM] * 2,
        out_shape=[
            jax.ShapeDtypeStruct((NZ, ROWS, PAIR), BF),
            jax.ShapeDtypeStruct((NX * NZ, 16, HD), BF),
        ],
        cost_estimate=cost(70_000_000, 4_000_000, 100_000),
        compiler_params=PARAMS,
    )(queries, states, *marks)


CHUNKS = 4
STEP = HEADS * HD // CHUNKS


def decay_rows(extra):
    extra = extra.astype(F32)
    return [extra[3 * j : 3 * j + 1] + extra[3 * j + 1 : 3 * j + 2] + extra[3 * j + 2 : 3 * j + 3] for j in range(2)]


def intra_kernel(sizes, q_hbm, k_hbm, v_hbm, extras_hbm, anc_hbm, m1, m2, m3, *refs):
    outs_hbm, weights_hbm, (parts, extras, tree, out, weights, sems) = refs[:NX], refs[NX], refs[NX + 1 :]
    me = lax.axis_index("head")
    x, _ = place()
    cuts = [pl.ds(c * STEP, STEP) for c in range(CHUNKS)]
    pairs = [(anc_hbm.at[me], tree), (extras_hbm, extras)]
    for cut in cuts:
        pairs += [(ref.at[0, :, cut], parts.at[n, :, cut]) for n, ref in enumerate((q_hbm, k_hbm, v_hbm))]
    pairs += [(m.at[pl.ds(NZ * NODES, 2 * COLS)], weights.at[n]) for n, m in enumerate((m1, m2, m3))]
    copies = run_copies(pairs, sems)
    node = lax.broadcasted_iota(jnp.int32, (NODES, HD), 0)
    lane = lax.broadcasted_iota(jnp.int32, (NODES, HD), 1)
    live = (node < sizes[me]).astype(F32)
    copies[0].wait()
    copies[1].wait()
    anc = tree[...].astype(F32)
    depth = jnp.sum(anc, axis=1, keepdims=True)
    depth_t = lax.dot_general(jnp.ones((8, NODES), BF), anc.astype(BF), NT, preferred_element_type=F32)[0:1]
    blocks = HD // NODES
    wide_anc = jnp.concatenate([anc] * blocks, axis=1)
    wide_gaps = jnp.concatenate([depth - depth_t] * blocks, axis=1)
    own = [lane // NODES == n for n in range(blocks)]
    mask = jnp.concatenate([jnp.where(m, wide_anc, 0.0) for m in own])
    gaps = jnp.concatenate([jnp.where(m, wide_gaps, 0.0) for m in own])
    quarter = HEADS // NX
    for c in range(CHUNKS):
        for n in range(3):
            copies[2 + 3 * c + n].wait()
        shift = lax.rem(c - x + NX, NX)
        for first in range(c * quarter, (c + 1) * quarter, blocks):
            heads = range(first, first + blocks)
            q, k, v = (jnp.concatenate([parts[n, :, h * HD : (h + 1) * HD] for h in heads]) for n in range(3))
            rates = [jnp.broadcast_to(decay_rows(extras[h // 2])[h % 2], (NODES, HD)) for h in heads]
            scores = lax.dot_general(q, k, NT, preferred_element_type=F32)
            mix = (scores * (mask * jnp.exp(-jnp.concatenate(rates) * gaps))).astype(BF)
            intra = jnp.dot(mix, v, preferred_element_type=F32)
            for n, h in enumerate(heads):
                near = h % quarter
                value = live * intra[n * NODES : (n + 1) * NODES]
                out[shift, :, near * HD : (near + 1) * HD] = value.astype(BF)
    for copy in copies[2 + 3 * CHUNKS :]:
        copy.wait()
    sends = [pltpu.make_async_copy(out.at[n], outs_hbm[n], sems.at[len(pairs) + n]) for n in range(NX)]
    sends.append(pltpu.make_async_copy(weights, weights_hbm, sems.at[len(pairs) + NX]))
    for send in sends:
        send.start()
    for send in sends:
        send.wait()


def intra_part(sizes, q, k, v, extras, anc, messages):
    return pl.pallas_call(
        intra_kernel,
        in_specs=[SMEM] + [HBM] * 8,
        out_specs=[HBM] * (NX + 1),
        out_shape=[jax.ShapeDtypeStruct((NODES, QUART), BF)] * NX
        + [jax.ShapeDtypeStruct((NX - 1, 2 * COLS, PAIR), BF)],
        scratch_shapes=[
            pltpu.VMEM((3, NODES, HEADS * HD), BF),
            pltpu.VMEM((NX * NZ, 16, HD), BF),
            pltpu.VMEM((NODES, NODES), jnp.int32),
            pltpu.VMEM((NX, NODES, QUART), BF),
            pltpu.VMEM((NX - 1, 2 * COLS, PAIR), BF),
            pltpu.SemaphoreType.DMA((2 + 3 * CHUNKS + 3 + NX + 1,)),
        ],
        cost_estimate=cost(100_000_000, 4_000_000, 200_000),
        compiler_params=WIDEST,
    )(sizes, q, k, v, extras, anc, *messages)


def merge_kernel(sizes, inter_hbm, gain_hbm, extras_hbm, anc_hbm, *refs):
    intras, gates, refs = refs[:NX], refs[NX : 2 * NX], refs[2 * NX :]
    out, inter_ref, gate_ref, gain, extras, tree, square_ref, sems = refs
    x, z = place()
    spots = [lax.rem(x - slot + NX, NX) for slot in range(NX)]
    pairs = [(inter_hbm, inter_ref), (extras_hbm.at[pl.ds(x * NZ, NZ)], extras)]
    pairs.append((gain_hbm.at[pl.ds(pl.multiple_of(x * 2 * NZ, 2 * NZ), 2 * NZ)], gain))
    for slot, xa in enumerate(spots):
        pairs.append((anc_hbm.at[xa * NZ + z], tree.at[slot]))
        pairs.append((gates[slot].at[pl.ds(0, NZ * NODES)], gate_ref.at[slot]))
    copies = run_copies(pairs, sems)
    node = lax.broadcasted_iota(jnp.int32, (NODES, HD), 0)
    lane = lax.broadcasted_iota(jnp.int32, (1, HD), 1)
    copies[1].wait()
    rates = jnp.zeros((1, HD), F32)
    for h in range(2 * NZ):
        rates = jnp.where(lane == h, decay_rows(extras[h // 2])[h % 2], rates)
    copies[0].wait()
    copies[2].wait()
    for slot, xa in enumerate(spots):
        rows = pl.ds(pl.multiple_of(xa * NODES, NODES), NODES)
        half = lax.div(xa, 2)
        near = lax.rem(xa, 2) * NODES
        for copy in copies[3 + 2 * slot : 5 + 2 * slot]:
            copy.wait()
        depth = jnp.sum(tree[slot].astype(F32), axis=1, keepdims=True)
        live = (node < sizes[xa * NZ + z]).astype(F32)
        fade = live * jnp.exp(-rates * depth)
        squares = jnp.zeros((NODES, HD), F32)
        for h in range(2 * NZ):
            lanes = slice((h % 2) * HD, (h % 2 + 1) * HD)
            inter = inter_ref[h // 2, rows, lanes].astype(F32)
            intra = intras[slot][:, h * HD : (h + 1) * HD].astype(F32)
            attn = (fade[:, h : h + 1] * inter + intra).astype(BF).astype(F32)
            squares = squares + attn * attn
            gate = gate_ref[slot, (h // 2) * NODES : (h // 2 + 1) * NODES, lanes].astype(F32)
            place_rows = pl.ds(pl.multiple_of(h * HROWS + near, NODES), NODES)
            out[half, place_rows, :] = (attn * gain[h : h + 1, :] / (1.0 + jnp.exp(-gate))).astype(BF)
        square_ref[rows, :] = squares
    ones = jnp.ones((16, HD), BF)
    total = jnp.zeros((16, ROWS), F32)
    for piece in split3(square_ref[...]):
        total = total + lax.dot_general(ones, piece.astype(BF), NT, preferred_element_type=F32)
    row = lax.broadcasted_iota(jnp.int32, (16, ROWS), 0)
    hi, mid, low = split3(total)
    tail = jnp.where(row == 0, hi, jnp.where(row == 1, mid, jnp.where(row == 2, low, 0.0))).astype(BF)
    for half in range(2):
        out[half, 16 * HROWS :, :] = tail


def merge(sizes, inter, gain, extras, anc, intras, gates):
    return pl.pallas_call(
        merge_kernel,
        in_specs=[SMEM] + [HBM] * 4 + [VMEM] * NX + [HBM] * NX,
        out_specs=VMEM,
        out_shape=jax.ShapeDtypeStruct((2, PIECE, HD), BF),
        scratch_shapes=[
            pltpu.VMEM((NZ, ROWS, PAIR), BF),
            pltpu.VMEM((NX, NZ * NODES, PAIR), BF),
            pltpu.VMEM((2 * NZ, HD), F32),
            pltpu.VMEM((NZ, 16, HD), BF),
            pltpu.VMEM((NX, NODES, NODES), jnp.int32),
            pltpu.VMEM((ROWS, HD), F32),
            pltpu.SemaphoreType.DMA((3 + 2 * NX,)),
        ],
        cost_estimate=cost(10_000_000, 4_000_000),
        compiler_params=PARAMS,
    )(sizes, inter, gain, extras, anc, *intras, *gates)


def project_kernel(halves, count, *refs):
    pieces, weights, outs, lhs = refs[:count], refs[count], refs[count + 1 : count + 1 + NX], refs[-1]
    pick = lax.broadcasted_iota(jnp.int32, (16, 64), 0) == lax.broadcasted_iota(jnp.int32, (16, 64), 1)
    pick = pick.astype(F32).astype(BF)
    for n, (ref, which, half) in enumerate(halves):
        piece = pieces[ref] if which is None else pieces[ref].at[which]
        rows = slice(n * HROWS, (n + 1) * HROWS)
        for h in range(2 * NZ):
            lhs[rows, h * HD : (h + 1) * HD] = piece[h * HROWS : (h + 1) * HROWS, :]
        sums = lax.dot_general(
            piece[16 * HROWS :, :], pick, (((0,), (0,)), ((), ())), preferred_element_type=F32
        )[half * HROWS : (half + 1) * HROWS]
        for out in outs:
            out[rows, COLS:] = sums.astype(out.dtype)
    for n, out in enumerate(outs):
        acc = lax.dot_general(lhs[...], weights[n], NT, preferred_element_type=F32)
        out[:, :COLS] = acc.astype(out.dtype)


def project(pieces, weights):
    halves = []
    for ref, piece in enumerate(pieces):
        if piece.ndim == 3:
            halves += [(ref, 0, 0), (ref, 1, 1)]
        else:
            halves.append((ref, None, ref))
    rows = len(halves) * HROWS
    return pl.pallas_call(
        functools.partial(project_kernel, halves, len(pieces)),
        in_specs=[VMEM] * (len(pieces) + 1),
        out_specs=[VMEM] * NX,
        out_shape=[jax.ShapeDtypeStruct((rows, 256), F32)] + [jax.ShapeDtypeStruct((rows, 256), BF)] * (NX - 1),
        scratch_shapes=[pltpu.VMEM((rows, QUART), BF)],
        cost_estimate=cost(2 * rows * QUART * COLS * NX, 4_000_000),
        compiler_params=PARAMS,
    )(*pieces, weights)


def finish_kernel(layout, *refs):
    out = refs[-1]
    _, z = place()
    for g, places in enumerate(layout):
        own, a, b, c = refs[4 * g : 4 * g + 4]
        row = 0
        for shift, first, last in places:
            size = (last - first) * NODES
            rows = slice(row, row + size)
            total = own[rows, :] + a[rows, :].astype(F32) + b[rows, :].astype(F32) + c[rows, :].astype(F32)
            squares = total[:, COLS : COLS + 1] + total[:, COLS + 1 : COLS + 2] + total[:, COLS + 2 : COLS + 3]
            scaled = total[:, :COLS] * lax.rsqrt(squares * (1.0 / (HEADS * HD)) + 1e-06)
            source = lax.rem(z - shift + 2 * NZ, NZ)
            for x in range(first, last):
                part = scaled[(x - first) * NODES : (x - first + 1) * NODES]
                out[x, source] = part.astype(BF)
            row += size


def finish(groups, layout):
    flat = [a for group in groups for a in group]
    return pl.pallas_call(
        functools.partial(finish_kernel, layout),
        in_specs=[VMEM] * len(flat),
        out_specs=VMEM,
        out_shape=jax.ShapeDtypeStruct((NX, NZ, NODES, COLS), BF),
        cost_estimate=cost(2_000_000, 4_000_000),
        compiler_params=PARAMS,
    )(*flat)


ZLINES = [[x * NZ + z for z in range(NZ)] for x in range(NX)]


def tie(arrays, *marks):
    return lax.optimization_barrier((*arrays, *marks))[: len(arrays)]


def per_device(queries, keys, values, gate, states, decay, ancestors, tree_sizes, gain, out_weight):
    packed = pack_queries(decay, queries)
    w0, m0, m1, m2, m3 = pack_messages(gate, out_weight.T, packed)
    m2, m1, m3 = xsend(m2, 2), xsend(m1, 1), xsend(m3, 3)
    spread = lax.all_to_all(packed, "head", 0, 0, tiled=True)
    inter, extras = inter_part(spread, states, [])
    (inter,) = tie((inter,), m1, m2, m3)
    inter = lax.all_to_all(inter, "head", 0, 0, axis_index_groups=ZLINES, tiled=True)
    t0, t1, t2, t3, mine = intra_part(tree_sizes, queries, keys, values, extras, ancestors, (m1, m2, m3))
    t2, t1, t3 = xsend(t2, 2), xsend(t1, 1), xsend(t3, 3)
    yours = swap_y(mine)
    gain = gain.reshape(HEADS, HD)
    own = merge(tree_sizes, inter, gain, extras, ancestors, (t0, t1, t2, t3), (m0, m1, m2, m3))
    theirs = swap_core(jnp.stack(tie((mine, yours), own)))
    weights = join_weights(w0, mine, yours, theirs)

    groups, layout = [], []

    def send_sums(pieces, places):
        own_part, *others = project(pieces, weights)
        groups.append([own_part] + [xsend(p, -d) for d, p in enumerate(others, 1)])
        layout.append(places)
        return own_part

    up, dn = zsend(own, 1), zsend(own, -1)
    mark = send_sums([own], [(0, 0, NX)])
    for step in range(1, 4):
        up, dn = tie((up, dn), *groups[-1])
        pieces = up, dn
        if step < 3:
            up, dn = zsend(up, 1), zsend(dn, -1)
        else:
            up, dn = zsend(up[0], 1), zsend(dn[1], -1)
        mark = send_sums(pieces, [(step, 0, NX), (-step, 0, NX)])
    last = tie((up, dn), mark)
    send_sums(last, [(4, 0, NX // 2), (-4, NX // 2, NX)])
    out = finish(groups, layout)
    return out.reshape(NX * NZ, NODES, COLS)


def solution(mesh):
    return jax.shard_map(
        per_device,
        mesh=mesh,
        in_specs=(
            P(("dp", "head"), None, None),
            P(("dp", "head"), None, None),
            P(("dp", "head"), None, None),
            P(("dp", "head"), None, None),
            P("dp", "head", None, None),
            P("head"),
            P("dp", None, None),
            P("dp"),
            P(),
            P(None, "head"),
        ),
        out_specs=P("dp", None, "head"),
        check_vma=False,
    )
```

```python
import functools
import jax
import jax.numpy as jnp
from jax import lax
from jax.experimental import pallas as pl
from jax.experimental.pallas import tpu as pltpu
from jax.sharding import PartitionSpec as P

NX = 4
NZ = 8
NODES = 32
HEADS = 64
HD = 128
PAIR = 2 * HD
QUART = 2048
PART = QUART // 4

NY = 4
COLS = 192
MSG = NODES * 8 + 2 * COLS
HROWS = 64
PIECE = 16 * HROWS + 16
ROWS = NX * NODES
EXTRA = 8
QROWS = 2 * NODES + EXTRA
NT = (((1,), (1,)), ((), ()))
BF = jnp.bfloat16
F32 = jnp.float32
ANY = pl.BlockSpec(memory_space=pl.ANY)
HBM = pl.BlockSpec(memory_space=pltpu.HBM)
VMEM = pl.BlockSpec(memory_space=pltpu.VMEM)
SMEM = pl.BlockSpec(memory_space=pltpu.SMEM)
WIDEST = pltpu.CompilerParams(vmem_limit_bytes=60 * 1024 * 1024)
PARAMS = pltpu.CompilerParams(vmem_limit_bytes=16 * 1024 * 1024)


def zsend(array, shift):
    pairs = [(x * NZ + z, x * NZ + (z + shift) % NZ) for x in range(NX) for z in range(NZ)]
    return lax.ppermute(array, "head", pairs)


def xsend(array, shift):
    pairs = [(x * NZ + z, ((x + shift) % NX) * NZ + z) for x in range(NX) for z in range(NZ)]
    return lax.ppermute(array, "head", pairs)


def swap_y(array):
    return lax.ppermute(array, "dp", [(i, i ^ 2) for i in range(2 * NY)])


def swap_core(array):
    return lax.ppermute(array, "dp", [(i, i ^ 1) for i in range(2 * NY)])


def place():
    me = lax.axis_index("head")
    return lax.div(me, NZ), lax.rem(me, NZ)


def cost(flops, size, trans=0):
    return pl.CostEstimate(flops=flops, bytes_accessed=size, transcendentals=trans)


def run_copies(pairs, sems):
    copies = [pltpu.make_async_copy(a, b, sems.at[n]) for n, (a, b) in enumerate(pairs)]
    for copy in copies:
        copy.start()
    return copies


def split3(value):
    hi = value.astype(BF).astype(F32)
    mid = (value - hi).astype(BF).astype(F32)
    return hi, mid, value - hi - mid


def pack_queries_kernel(decay, q_hbm, out, q, sems):
    cuts = [slice(n * QUART, (n + 1) * QUART) for n in range(NX)]
    copies = run_copies([(q_hbm.at[0, :, cut], q.at[:, cut]) for cut in cuts], sems)
    row = lax.broadcasted_iota(jnp.int32, (EXTRA, HD), 0)
    rows = jnp.zeros((EXTRA, HD), F32)
    for j in range(2):
        for n, piece in enumerate(split3(jnp.full((EXTRA, HD), decay[j], F32))):
            rows = jnp.where(row == 3 * j + n, piece, rows)
    tail = rows.astype(BF)
    for n in range(NX * NZ):
        out[n, 2 * NODES :, :] = tail
    for n in range(NX * NZ):
        if n % NZ == 0:
            copies[n // NZ].wait()
        for j in range(2):
            out[n, j * NODES : (j + 1) * NODES, :] = q[:, (2 * n + j) * HD : (2 * n + j + 1) * HD]


def pack_queries(decay, q):
    return pl.pallas_call(
        pack_queries_kernel,
        in_specs=[SMEM, HBM],
        out_specs=VMEM,
        out_shape=jax.ShapeDtypeStruct((NX * NZ, QROWS, HD), BF),
        scratch_shapes=[pltpu.VMEM((NODES, HEADS * HD), BF), pltpu.SemaphoreType.DMA((NX,))],
        cost_estimate=cost(0, 1_000_000),
        compiler_params=WIDEST,
    )(decay, q)


def pack_messages_kernel(gate_hbm, w, after, w0_hbm, *refs):
    outs_hbm, (gate, w0, outs, sems) = refs[:NX], refs[NX:]
    x, _ = place()
    cuts = [slice(n * QUART, (n + 1) * QUART) for n in range(NX)]
    pairs = [(gate_hbm.at[0, :, cut], gate.at[:, cut]) for cut in cuts]
    bases = [lax.rem(x + n, NX) * QUART for n in range(NX)]
    for n in (2, 1, 3):
        for b in range(2):
            col = pl.multiple_of(bases[n] + lax.rem(lax.axis_index("dp"), 4) * PART + b * PAIR, PAIR)
            pairs.append((w.at[:, pl.ds(col, PAIR)], outs.at[n, pl.ds(NZ * NODES + b * COLS, COLS)]))
    pairs.append((w.at[:, pl.ds(pl.multiple_of(x * QUART, QUART), QUART)], w0))
    copies = run_copies(pairs, sems)
    for copy in copies[:NX]:
        copy.wait()
    sends = []
    for i, n in enumerate((2, 1, 3, 0)):
        for b in range(NZ):
            cols = pl.ds(pl.multiple_of(bases[n] + b * PAIR, PAIR), PAIR)
            outs[n, b * NODES : (b + 1) * NODES, :] = gate[:, cols]
        rows = pl.ds(0, NZ * NODES)
        if n:
            copies[NX + 2 * i].wait()
            copies[NX + 2 * i + 1].wait()
            rows = pl.ds(0, MSG)
        sends.append(pltpu.make_async_copy(outs.at[n, rows], outs_hbm[n].at[rows], sems.at[len(pairs) + n]))
        sends[-1].start()
    copies[-1].wait()
    sends.append(pltpu.make_async_copy(w0, w0_hbm, sems.at[len(pairs) + NX]))
    sends[-1].start()
    for send in sends:
        send.wait()


def pack_messages(gate, w, after):
    return pl.pallas_call(
        pack_messages_kernel,
        in_specs=[HBM] * 2 + [ANY],
        out_specs=[HBM] * (1 + NX),
        out_shape=[jax.ShapeDtypeStruct((COLS, QUART), BF)] + [jax.ShapeDtypeStruct((NZ * NODES, PAIR), BF)]
        + [jax.ShapeDtypeStruct((MSG, PAIR), BF)] * (NX - 1),
        scratch_shapes=[
            pltpu.VMEM((NODES, HEADS * HD), BF),
            pltpu.VMEM((COLS, QUART), BF),
            pltpu.VMEM((NX, MSG, PAIR), BF),
            pltpu.SemaphoreType.DMA((NX + 7 + NX + 1,)),
        ],
        cost_estimate=cost(0, 4_000_000),
        compiler_params=WIDEST,
    )(gate, w, after)


def join_weights_kernel(w0, m0, m1, theirs, out):
    part = lax.rem(lax.axis_index("dp"), 4)
    flip = 1 - 2 * lax.rem(part, 2)
    far = lax.rem(part + 2, 4)
    out[:COLS, :] = w0[...]
    for s, (ref, mine) in enumerate(((m0, part), (m1, far))):
        for d in range(NX - 1):
            for b in range(2):
                near = pl.ds(pl.multiple_of(mine * PART + b * PAIR, PAIR), PAIR)
                other = pl.ds(pl.multiple_of((mine + flip) * PART + b * PAIR, PAIR), PAIR)
                out[(d + 1) * COLS : (d + 2) * COLS, near] = ref[d, b * COLS : (b + 1) * COLS]
                out[(d + 1) * COLS : (d + 2) * COLS, other] = theirs[s, d, b * COLS : (b + 1) * COLS]


def join_weights(w0, m0, m1, theirs):
    return pl.pallas_call(
        join_weights_kernel,
        in_specs=[VMEM] * 4,
        out_specs=VMEM,
        out_shape=jax.ShapeDtypeStruct((NX * COLS, QUART), BF),
        cost_estimate=cost(0, 6_000_000),
        compiler_params=PARAMS,
    )(w0, m0, m1, theirs)


def inter_kernel(queries, states, *refs):
    out, extras = refs[-2:]
    for r in range(NX * NZ):
        x, z = divmod(r, NZ)
        for j in range(2):
            rows = slice(j * NODES, (j + 1) * NODES)
            inter = jnp.dot(queries[r, rows, :], states[r, j], preferred_element_type=F32)
            out[z, x * NODES : (x + 1) * NODES, j * HD : (j + 1) * HD] = inter.astype(BF)
        extras[r] = queries[r, 2 * NODES :, :]


def inter_part(queries, states, marks):
    return pl.pallas_call(
        inter_kernel,
        in_specs=[VMEM] * 2 + [ANY] * len(marks),
        out_specs=[VMEM] * 2,
        out_shape=[
            jax.ShapeDtypeStruct((NZ, ROWS, PAIR), BF),
            jax.ShapeDtypeStruct((NX * NZ, EXTRA, HD), BF),
        ],
        cost_estimate=cost(70_000_000, 4_000_000, 100_000),
        compiler_params=PARAMS,
    )(queries, states, *marks)


CHUNKS = 4
STEP = HEADS * HD // CHUNKS


def decay_rows(extra):
    extra = extra.astype(F32)
    return [extra[3 * j : 3 * j + 1] + extra[3 * j + 1 : 3 * j + 2] + extra[3 * j + 2 : 3 * j + 3] for j in range(2)]


def intra_kernel(sizes, q_hbm, k_hbm, v_hbm, extras_hbm, anc_hbm, m0, m1, m2, m3, *refs):
    outs_hbm, refs = refs[:NX], refs[NX:]
    weights_hbm, gates_hbm, parts, extras, tree, out, weights, gates, sems = refs
    me = lax.axis_index("head")
    x, _ = place()
    cuts = [pl.ds(c * STEP, STEP) for c in range(CHUNKS)]
    pairs = [(anc_hbm.at[me], tree), (extras_hbm, extras)]
    for cut in cuts:
        pairs += [(ref.at[0, :, cut], parts.at[n, :, cut]) for n, ref in enumerate((q_hbm, k_hbm, v_hbm))]
    pairs += [(m.at[pl.ds(NZ * NODES, 2 * COLS)], weights.at[n]) for n, m in enumerate((m1, m2, m3))]
    pairs += [(m.at[pl.ds(0, NZ * NODES)], gates.at[n]) for n, m in enumerate((m0, m1, m2, m3))]
    copies = run_copies(pairs, sems)
    node = lax.broadcasted_iota(jnp.int32, (NODES, HD), 0)
    lane = lax.broadcasted_iota(jnp.int32, (NODES, HD), 1)
    live = (node < sizes[me]).astype(F32)
    copies[0].wait()
    copies[1].wait()
    anc = tree[...].astype(F32)
    depth = jnp.sum(anc, axis=1, keepdims=True)
    depth_t = lax.dot_general(jnp.ones((8, NODES), BF), anc.astype(BF), NT, preferred_element_type=F32)[0:1]
    blocks = HD // NODES
    wide_anc = jnp.concatenate([anc] * blocks, axis=1)
    wide_gaps = jnp.concatenate([depth - depth_t] * blocks, axis=1)
    own = [lane // NODES == n for n in range(blocks)]
    mask = jnp.concatenate([jnp.where(m, wide_anc, 0.0) for m in own])
    gaps = jnp.concatenate([jnp.where(m, wide_gaps, 0.0) for m in own])
    quarter = HEADS // NX
    for c in range(CHUNKS):
        for n in range(3):
            copies[2 + 3 * c + n].wait()
        shift = lax.rem(c - x + NX, NX)
        for first in range(c * quarter, (c + 1) * quarter, blocks):
            heads = range(first, first + blocks)
            q, k, v = (jnp.concatenate([parts[n, :, h * HD : (h + 1) * HD] for h in heads]) for n in range(3))
            rates = [jnp.broadcast_to(decay_rows(extras[h // 2])[h % 2], (NODES, HD)) for h in heads]
            scores = lax.dot_general(q, k, NT, preferred_element_type=F32)
            mix = (scores * (mask * jnp.exp(-jnp.concatenate(rates) * gaps))).astype(BF)
            intra = jnp.dot(mix, v, preferred_element_type=F32)
            for n, h in enumerate(heads):
                near = h % quarter
                value = live * intra[n * NODES : (n + 1) * NODES]
                out[shift, :, near * HD : (near + 1) * HD] = value.astype(BF)
    for copy in copies[2 + 3 * CHUNKS :]:
        copy.wait()
    sends = [pltpu.make_async_copy(out.at[n], outs_hbm[n], sems.at[len(pairs) + n]) for n in range(NX)]
    sends.append(pltpu.make_async_copy(weights, weights_hbm, sems.at[len(pairs) + NX]))
    sends.append(pltpu.make_async_copy(gates, gates_hbm, sems.at[len(pairs) + NX + 1]))
    for send in sends:
        send.start()
    for send in sends:
        send.wait()


def intra_part(sizes, q, k, v, extras, anc, messages):
    return pl.pallas_call(
        intra_kernel,
        in_specs=[SMEM] + [HBM] * 9,
        out_specs=[HBM] * (NX + 2),
        out_shape=[jax.ShapeDtypeStruct((NODES, QUART), BF)] * NX
        + [jax.ShapeDtypeStruct((NX - 1, 2 * COLS, PAIR), BF), jax.ShapeDtypeStruct((NX, NZ * NODES, PAIR), BF)],
        scratch_shapes=[
            pltpu.VMEM((3, NODES, HEADS * HD), BF),
            pltpu.VMEM((NX * NZ, EXTRA, HD), BF),
            pltpu.VMEM((NODES, NODES), jnp.int32),
            pltpu.VMEM((NX, NODES, QUART), BF),
            pltpu.VMEM((NX - 1, 2 * COLS, PAIR), BF),
            pltpu.VMEM((NX, NZ * NODES, PAIR), BF),
            pltpu.SemaphoreType.DMA((2 + 3 * CHUNKS + 7 + NX + 2,)),
        ],
        cost_estimate=cost(100_000_000, 4_000_000, 200_000),
        compiler_params=WIDEST,
    )(sizes, q, k, v, extras, anc, *messages)


def merge_kernel(sizes, inter_hbm, gain_hbm, extras_hbm, anc_hbm, *refs):
    intras, gates, refs = refs[:NX], refs[NX], refs[NX + 1 :]
    out, inter_ref, gate_ref, gain, extras, tree, square_ref, sems = refs
    x, z = place()
    spots = [lax.rem(x - slot + NX, NX) for slot in range(NX)]
    pairs = [(inter_hbm, inter_ref), (extras_hbm.at[pl.ds(x * NZ, NZ)], extras)]
    pairs.append((gain_hbm.at[pl.ds(pl.multiple_of(x * 2 * NZ, 2 * NZ), 2 * NZ)], gain))
    for slot, xa in enumerate(spots):
        pairs.append((anc_hbm.at[xa * NZ + z], tree.at[slot]))
        pairs.append((gates.at[slot], gate_ref.at[slot]))
    copies = run_copies(pairs, sems)
    node = lax.broadcasted_iota(jnp.int32, (NODES, HD), 0)
    lane = lax.broadcasted_iota(jnp.int32, (1, HD), 1)
    copies[1].wait()
    rates = jnp.zeros((1, HD), F32)
    for h in range(2 * NZ):
        rates = jnp.where(lane == h, decay_rows(extras[h // 2])[h % 2], rates)
    copies[0].wait()
    copies[2].wait()
    for slot, xa in enumerate(spots):
        rows = pl.ds(pl.multiple_of(xa * NODES, NODES), NODES)
        half = lax.div(xa, 2)
        near = lax.rem(xa, 2) * NODES
        for copy in copies[3 + 2 * slot : 5 + 2 * slot]:
            copy.wait()
        depth = jnp.sum(tree[slot].astype(F32), axis=1, keepdims=True)
        live = (node < sizes[xa * NZ + z]).astype(F32)
        fade = live * jnp.exp(-rates * depth)
        squares = jnp.zeros((NODES, HD), F32)
        for h in range(2 * NZ):
            lanes = slice((h % 2) * HD, (h % 2 + 1) * HD)
            inter = inter_ref[h // 2, rows, lanes].astype(F32)
            intra = intras[slot][:, h * HD : (h + 1) * HD].astype(F32)
            attn = (fade[:, h : h + 1] * inter + intra).astype(BF).astype(F32)
            squares = squares + attn * attn
            gate = gate_ref[slot, (h // 2) * NODES : (h // 2 + 1) * NODES, lanes].astype(F32)
            place_rows = pl.ds(pl.multiple_of(h * HROWS + near, NODES), NODES)
            out[half, place_rows, :] = (attn * gain[h : h + 1, :] / (1.0 + jnp.exp(-gate))).astype(BF)
        square_ref[rows, :] = squares
    ones = jnp.ones((16, HD), BF)
    total = jnp.zeros((16, ROWS), F32)
    for piece in split3(square_ref[...]):
        total = total + lax.dot_general(ones, piece.astype(BF), NT, preferred_element_type=F32)
    row = lax.broadcasted_iota(jnp.int32, (16, ROWS), 0)
    hi, mid, low = split3(total)
    tail = jnp.where(row == 0, hi, jnp.where(row == 1, mid, jnp.where(row == 2, low, 0.0))).astype(BF)
    for half in range(2):
        out[half, 16 * HROWS :, :] = tail


def merge(sizes, inter, gain, extras, anc, intras, gates):
    return pl.pallas_call(
        merge_kernel,
        in_specs=[SMEM] + [HBM] * 4 + [VMEM] * NX + [HBM],
        out_specs=VMEM,
        out_shape=jax.ShapeDtypeStruct((2, PIECE, HD), BF),
        scratch_shapes=[
            pltpu.VMEM((NZ, ROWS, PAIR), BF),
            pltpu.VMEM((NX, NZ * NODES, PAIR), BF),
            pltpu.VMEM((2 * NZ, HD), F32),
            pltpu.VMEM((NZ, EXTRA, HD), BF),
            pltpu.VMEM((NX, NODES, NODES), jnp.int32),
            pltpu.VMEM((ROWS, HD), F32),
            pltpu.SemaphoreType.DMA((3 + 2 * NX,)),
        ],
        cost_estimate=cost(10_000_000, 4_000_000),
        compiler_params=PARAMS,
    )(sizes, inter, gain, extras, anc, *intras, gates)


def project_kernel(count, *refs):
    pieces, weights, outs, u = refs[:count], refs[count], refs[count + 1 : count + 1 + NX], refs[-1]
    if len(pieces[0].shape) == 3:
        halves = [piece.at[half] for piece in pieces for half in range(2)]
        tails = [piece[0, 16 * HROWS :, :] for piece in pieces]
    else:
        halves = pieces
        lane = lax.broadcasted_iota(jnp.int32, (16, ROWS), 1)
        first, second = (piece[16 * HROWS :, :].astype(F32) for piece in pieces)
        tails = [jnp.where(lane < HROWS, first, second).astype(BF)]
    for n, half in enumerate(halves):
        for h in range(2 * NZ):
            u[n * HROWS : (n + 1) * HROWS, h * HD : (h + 1) * HD] = half[h * HROWS : (h + 1) * HROWS, :]
    acc = lax.dot_general(weights[...], u[...], NT, preferred_element_type=F32)
    for n, out in enumerate(outs):
        out[:COLS, :] = acc[n * COLS : (n + 1) * COLS].astype(out.dtype)
        for p, tail in enumerate(tails):
            out[COLS:, p * ROWS : (p + 1) * ROWS] = tail.astype(out.dtype)


def project(pieces, weights):
    rows = ROWS * len(pieces) if pieces[0].ndim == 3 else ROWS
    shape = (COLS + 16, rows)
    return pl.pallas_call(
        functools.partial(project_kernel, len(pieces)),
        in_specs=[VMEM] * (len(pieces) + 1),
        out_specs=[VMEM] * NX,
        out_shape=[jax.ShapeDtypeStruct(shape, F32)] + [jax.ShapeDtypeStruct(shape, BF)] * (NX - 1),
        scratch_shapes=[pltpu.VMEM((rows, QUART), BF)],
        cost_estimate=cost(2 * rows * QUART * COLS * NX, 4_000_000),
        compiler_params=PARAMS,
    )(*pieces, weights)


def finish_kernel(layout, *refs):
    out_hbm, out, sems = refs[-3:]
    _, z = place()
    sends = []
    for g, shifts in enumerate(layout):
        parts = refs[4 * g : 4 * g + 4]
        for p, shift in enumerate(shifts):
            cols = slice(p * ROWS, (p + 1) * ROWS)
            total = sum(part[:, cols].astype(F32) for part in parts)
            squares = total[COLS : COLS + 1] + total[COLS + 1 : COLS + 2] + total[COLS + 2 : COLS + 3]
            scaled = total[:COLS] * lax.rsqrt(squares * (1.0 / (HEADS * HD)) + 1e-06)
            rest = jnp.concatenate([scaled[HD:], jnp.zeros((2 * HD - COLS, ROWS), F32)])
            left, right = scaled[:HD].T, rest.T
            source = lax.rem(z - shift + 2 * NZ, NZ)
            for x in range(NX):
                n = len(sends)
                rows = slice(x * NODES, (x + 1) * NODES)
                out[n, :, :HD] = left[rows].astype(BF)
                out[n, :, HD:] = right[rows, : COLS - HD].astype(BF)
                sends.append(pltpu.make_async_copy(out.at[n], out_hbm.at[x, source], sems.at[n]))
                sends[-1].start()
    for send in sends:
        send.wait()


def finish(groups, layout, before=None):
    flat = [a for group in groups for a in group]
    blocks = NX * sum(len(shifts) for shifts in layout)
    extra = [] if before is None else [before]
    return pl.pallas_call(
        functools.partial(finish_kernel, layout),
        in_specs=[VMEM] * len(flat) + [HBM] * len(extra),
        out_specs=HBM,
        out_shape=jax.ShapeDtypeStruct((NX, NZ, NODES, COLS), BF),
        scratch_shapes=[pltpu.VMEM((blocks, NODES, COLS), BF), pltpu.SemaphoreType.DMA((blocks,))],
        input_output_aliases={len(flat): 0} if extra else {},
        cost_estimate=cost(2_000_000, 4_000_000),
        compiler_params=PARAMS,
    )(*flat, *extra)


ZLINES = [[x * NZ + z for z in range(NZ)] for x in range(NX)]


def tie(arrays, *marks):
    return lax.optimization_barrier((*arrays, *marks))[: len(arrays)]


def per_device(queries, keys, values, gate, states, decay, ancestors, tree_sizes, gain, out_weight):
    packed = pack_queries(decay, queries)
    w0, m0, m1, m2, m3 = pack_messages(gate, out_weight.T, packed)
    m2, m1, m3 = xsend(m2, 2), xsend(m1, 1), xsend(m3, 3)
    spread = lax.all_to_all(packed, "head", 0, 0, tiled=True)
    inter, extras = inter_part(spread, states, [])
    (inter,) = tie((inter,), m2, m1, m3)
    inter = lax.all_to_all(inter, "head", 0, 0, axis_index_groups=ZLINES, tiled=True)
    messages = (m0, m1, m2, m3)
    t0, t1, t2, t3, mine, gates = intra_part(tree_sizes, queries, keys, values, extras, ancestors, messages)
    t2, t1, t3 = xsend(t2, 2), xsend(t1, 1), xsend(t3, 3)
    yours = swap_y(mine)
    gain = gain.reshape(HEADS, HD)
    own = merge(tree_sizes, inter, gain, extras, ancestors, (t0, t1, t2, t3), gates)
    theirs = swap_core(jnp.stack(tie((mine, yours), own)))
    weights = join_weights(w0, mine, yours, theirs)

    groups, layout = [], []

    def send_sums(pieces, places):
        own_part, *others = project(pieces, weights)
        groups.append([own_part] + [xsend(p, -d) for d, p in enumerate(others, 1)])
        layout.append(places)
        return own_part

    up, dn = zsend(own, 1), zsend(own, -1)
    mark = send_sums([own], [0])
    for step in range(1, 4):
        up, dn = tie((up, dn), *groups[-1])
        pieces = up, dn
        if step < 3:
            up, dn = zsend(up, 1), zsend(dn, -1)
        else:
            up, dn = zsend(up[0], 1), zsend(dn[1], -1)
        mark = send_sums(pieces, [step, -step])
    last = tie((up, dn), mark)
    send_sums(last, [4])
    out = finish(groups[:3], layout[:3])
    out = finish(groups[3:], layout[3:], out)
    return out.reshape(NX * NZ, NODES, COLS)


def solution(mesh):
    return jax.shard_map(
        per_device,
        mesh=mesh,
        in_specs=(
            P(("dp", "head"), None, None),
            P(("dp", "head"), None, None),
            P(("dp", "head"), None, None),
            P(("dp", "head"), None, None),
            P("dp", "head", None, None),
            P("head"),
            P("dp", None, None),
            P("dp"),
            P(),
            P(None, "head"),
        ),
        out_specs=P("dp", None, "head"),
        check_vma=False,
    )
```

```python
import functools
import jax
import jax.numpy as jnp
from jax import lax
from jax.experimental import pallas as pl
from jax.experimental.pallas import tpu as pltpu
from jax.sharding import PartitionSpec as P

NX = 4
NZ = 8
NODES = 32
HEADS = 64
HD = 128
PAIR = 2 * HD
QUART = 2048
PART = QUART // 4

NY = 4
COLS = 192
MSG = NODES * 8 + 2 * COLS
HROWS = 64
PIECE = 16 * HROWS + 16
ROWS = NX * NODES
EXTRA = 8
QROWS = 2 * NODES + EXTRA
NT = (((1,), (1,)), ((), ()))
BF = jnp.bfloat16
F32 = jnp.float32
ANY = pl.BlockSpec(memory_space=pl.ANY)
HBM = pl.BlockSpec(memory_space=pltpu.HBM)
VMEM = pl.BlockSpec(memory_space=pltpu.VMEM)
SMEM = pl.BlockSpec(memory_space=pltpu.SMEM)
WIDEST = pltpu.CompilerParams(vmem_limit_bytes=60 * 1024 * 1024)
PARAMS = pltpu.CompilerParams(vmem_limit_bytes=16 * 1024 * 1024)


def zsend(array, shift):
    pairs = [(x * NZ + z, x * NZ + (z + shift) % NZ) for x in range(NX) for z in range(NZ)]
    return lax.ppermute(array, "head", pairs)


def xsend(array, shift):
    pairs = [(x * NZ + z, ((x + shift) % NX) * NZ + z) for x in range(NX) for z in range(NZ)]
    return lax.ppermute(array, "head", pairs)


def swap_y(array):
    return lax.ppermute(array, "dp", [(i, i ^ 2) for i in range(2 * NY)])


def swap_core(array):
    return lax.ppermute(array, "dp", [(i, i ^ 1) for i in range(2 * NY)])


def place():
    me = lax.axis_index("head")
    return lax.div(me, NZ), lax.rem(me, NZ)


def cost(flops, size, trans=0):
    return pl.CostEstimate(flops=flops, bytes_accessed=size, transcendentals=trans)


def run_copies(pairs, sems):
    copies = [pltpu.make_async_copy(a, b, sems.at[n]) for n, (a, b) in enumerate(pairs)]
    for copy in copies:
        copy.start()
    return copies


def split3(value):
    hi = value.astype(BF).astype(F32)
    mid = (value - hi).astype(BF).astype(F32)
    return hi, mid, value - hi - mid


def pack_queries_kernel(decay, q_hbm, out, q, sems):
    cuts = [slice(n * QUART, (n + 1) * QUART) for n in range(NX)]
    copies = run_copies([(q_hbm.at[0, :, cut], q.at[:, cut]) for cut in cuts], sems)
    row = lax.broadcasted_iota(jnp.int32, (EXTRA, HD), 0)
    rows = jnp.zeros((EXTRA, HD), F32)
    for j in range(2):
        for n, piece in enumerate(split3(jnp.full((EXTRA, HD), decay[j], F32))):
            rows = jnp.where(row == 3 * j + n, piece, rows)
    tail = rows.astype(BF)
    for n in range(NX * NZ):
        out[n, 2 * NODES :, :] = tail
    for n in range(NX * NZ):
        if n % NZ == 0:
            copies[n // NZ].wait()
        for j in range(2):
            out[n, j * NODES : (j + 1) * NODES, :] = q[:, (2 * n + j) * HD : (2 * n + j + 1) * HD]


def pack_queries(decay, q):
    return pl.pallas_call(
        pack_queries_kernel,
        in_specs=[SMEM, HBM],
        out_specs=VMEM,
        out_shape=jax.ShapeDtypeStruct((NX * NZ, QROWS, HD), BF),
        scratch_shapes=[pltpu.VMEM((NODES, HEADS * HD), BF), pltpu.SemaphoreType.DMA((NX,))],
        cost_estimate=cost(0, 1_000_000),
        compiler_params=WIDEST,
    )(decay, q)


def pack_messages_kernel(gate_hbm, w, after, *refs):
    outs_hbm, (gate, outs, sems) = refs[:NX], refs[NX:]
    x, _ = place()
    cuts = [slice(n * QUART, (n + 1) * QUART) for n in range(NX)]
    pairs = [(gate_hbm.at[0, :, cut], gate.at[:, cut]) for cut in cuts]
    bases = [lax.rem(x + n, NX) * QUART for n in range(NX)]
    for n in (2, 1, 3):
        for b in range(2):
            col = pl.multiple_of(bases[n] + lax.rem(lax.axis_index("dp"), 4) * PART + b * PAIR, PAIR)
            pairs.append((w.at[:, pl.ds(col, PAIR)], outs.at[n, pl.ds(NZ * NODES + b * COLS, COLS)]))
    copies = run_copies(pairs, sems)
    for copy in copies[:NX]:
        copy.wait()
    sends = []
    for i, n in enumerate((2, 1, 3, 0)):
        for b in range(NZ):
            cols = pl.ds(pl.multiple_of(bases[n] + b * PAIR, PAIR), PAIR)
            outs[n, b * NODES : (b + 1) * NODES, :] = gate[:, cols]
        rows = pl.ds(0, NZ * NODES)
        if n:
            copies[NX + 2 * i].wait()
            copies[NX + 2 * i + 1].wait()
            rows = pl.ds(0, MSG)
        sends.append(pltpu.make_async_copy(outs.at[n, rows], outs_hbm[n].at[rows], sems.at[len(pairs) + n]))
        sends[-1].start()
    for send in sends:
        send.wait()


def pack_messages(gate, w, after):
    return pl.pallas_call(
        pack_messages_kernel,
        in_specs=[HBM] * 2 + [ANY],
        out_specs=[HBM] * NX,
        out_shape=[jax.ShapeDtypeStruct((NZ * NODES, PAIR), BF)]
        + [jax.ShapeDtypeStruct((MSG, PAIR), BF)] * (NX - 1),
        scratch_shapes=[
            pltpu.VMEM((NODES, HEADS * HD), BF),
            pltpu.VMEM((NX, MSG, PAIR), BF),
            pltpu.SemaphoreType.DMA((NX + 6 + NX,)),
        ],
        cost_estimate=cost(0, 4_000_000),
        compiler_params=WIDEST,
    )(gate, w, after)


def join_weights_kernel(w0, m0, m1, theirs, out):
    part = lax.rem(lax.axis_index("dp"), 4)
    flip = 1 - 2 * lax.rem(part, 2)
    far = lax.rem(part + 2, 4)
    out[:COLS, :] = w0[...]
    for s, (ref, mine) in enumerate(((m0, part), (m1, far))):
        for d in range(NX - 1):
            for b in range(2):
                near = pl.ds(pl.multiple_of(mine * PART + b * PAIR, PAIR), PAIR)
                other = pl.ds(pl.multiple_of((mine + flip) * PART + b * PAIR, PAIR), PAIR)
                out[(d + 1) * COLS : (d + 2) * COLS, near] = ref[d, b * COLS : (b + 1) * COLS]
                out[(d + 1) * COLS : (d + 2) * COLS, other] = theirs[s, d, b * COLS : (b + 1) * COLS]


def join_weights(w0, m0, m1, theirs):
    return pl.pallas_call(
        join_weights_kernel,
        in_specs=[VMEM] * 4,
        out_specs=VMEM,
        out_shape=jax.ShapeDtypeStruct((NX * COLS, QUART), BF),
        cost_estimate=cost(0, 6_000_000),
        compiler_params=PARAMS,
    )(w0, m0, m1, theirs)


def inter_kernel(queries, states, *refs):
    out, extras = refs[-2:]
    for r in range(NX * NZ):
        x, z = divmod(r, NZ)
        for j in range(2):
            rows = slice(j * NODES, (j + 1) * NODES)
            inter = jnp.dot(queries[r, rows, :], states[r, j], preferred_element_type=F32)
            out[z, x * NODES : (x + 1) * NODES, j * HD : (j + 1) * HD] = inter.astype(BF)
        extras[r] = queries[r, 2 * NODES :, :]


def inter_part(queries, states, marks):
    return pl.pallas_call(
        inter_kernel,
        in_specs=[VMEM] * 2 + [ANY] * len(marks),
        out_specs=[VMEM] * 2,
        out_shape=[
            jax.ShapeDtypeStruct((NZ, ROWS, PAIR), BF),
            jax.ShapeDtypeStruct((NX * NZ, EXTRA, HD), BF),
        ],
        cost_estimate=cost(70_000_000, 4_000_000, 100_000),
        compiler_params=PARAMS,
    )(queries, states, *marks)


def decay_rows(extra):
    extra = extra.astype(F32)
    return [extra[3 * j : 3 * j + 1] + extra[3 * j + 1 : 3 * j + 2] + extra[3 * j + 2 : 3 * j + 3] for j in range(2)]


def intra_kernel(sizes, q_hbm, k_hbm, v_hbm, extras_hbm, anc_hbm, m1, m2, m3, *refs):
    outs_hbm, (weights_hbm, parts, extras, tree, out, weights, sems) = refs[:NX], refs[NX:]
    me = lax.axis_index("head")
    x, _ = place()
    order = (2, 1, 3, 0)
    quarters = [lax.rem(x + n, NX) for n in order]
    pairs = [(anc_hbm.at[me], tree), (extras_hbm, extras)]
    for n, quarter in zip(order, quarters):
        cut = pl.ds(pl.multiple_of(quarter * QUART, QUART), QUART)
        pairs += [(ref.at[0, :, cut], parts.at[n, i]) for i, ref in enumerate((q_hbm, k_hbm, v_hbm))]
    pairs += [(m.at[pl.ds(NZ * NODES, 2 * COLS)], weights.at[n]) for n, m in enumerate((m1, m2, m3))]
    copies = run_copies(pairs, sems)
    node = lax.broadcasted_iota(jnp.int32, (NODES, HD), 0)
    lane = lax.broadcasted_iota(jnp.int32, (NODES, HD), 1)
    live = (node < sizes[me]).astype(F32)
    copies[0].wait()
    copies[1].wait()
    anc = tree[...].astype(F32)
    depth = jnp.sum(anc, axis=1, keepdims=True)
    depth_t = lax.dot_general(jnp.ones((8, NODES), BF), anc.astype(BF), NT, preferred_element_type=F32)[0:1]
    blocks = HD // NODES
    wide_anc = jnp.concatenate([anc] * blocks, axis=1)
    wide_gaps = jnp.concatenate([depth - depth_t] * blocks, axis=1)
    own = [lane // NODES == n for n in range(blocks)]
    mask = jnp.concatenate([jnp.where(m, wide_anc, 0.0) for m in own])
    gaps = jnp.concatenate([jnp.where(m, wide_gaps, 0.0) for m in own])
    sends = []
    for i, (shift, quarter) in enumerate(zip(order, quarters)):
        for n in range(3):
            copies[2 + 3 * i + n].wait()
        for first in range(0, 2 * NZ, blocks):
            heads = range(first, first + blocks)
            q, k, v = (jnp.concatenate([parts[shift, n, :, h * HD : (h + 1) * HD] for h in heads]) for n in range(3))
            rates = []
            for h in heads:
                rate = decay_rows(extras[quarter * NZ + h // 2])[h % 2]
                rates.append(jnp.broadcast_to(rate, (NODES, HD)))
            scores = lax.dot_general(q, k, NT, preferred_element_type=F32)
            mix = (scores * (mask * jnp.exp(-jnp.concatenate(rates) * gaps))).astype(BF)
            intra = jnp.dot(mix, v, preferred_element_type=F32)
            for n, h in enumerate(heads):
                out[shift, :, h * HD : (h + 1) * HD] = (live * intra[n * NODES : (n + 1) * NODES]).astype(BF)
        sends.append(pltpu.make_async_copy(out.at[shift], outs_hbm[shift], sems.at[len(pairs) + shift]))
        sends[-1].start()
        if i == 1:
            for copy in copies[2 + 3 * NX :]:
                copy.wait()
            sends.append(pltpu.make_async_copy(weights, weights_hbm, sems.at[len(pairs) + NX]))
            sends[-1].start()
    for send in sends:
        send.wait()


def intra_part(sizes, q, k, v, extras, anc, messages):
    return pl.pallas_call(
        intra_kernel,
        in_specs=[SMEM] + [HBM] * 8,
        out_specs=[HBM] * (NX + 1),
        out_shape=[jax.ShapeDtypeStruct((NODES, QUART), BF)] * NX
        + [jax.ShapeDtypeStruct((NX - 1, 2 * COLS, PAIR), BF)],
        scratch_shapes=[
            pltpu.VMEM((NX, 3, NODES, QUART), BF),
            pltpu.VMEM((NX * NZ, EXTRA, HD), BF),
            pltpu.VMEM((NODES, NODES), jnp.int32),
            pltpu.VMEM((NX, NODES, QUART), BF),
            pltpu.VMEM((NX - 1, 2 * COLS, PAIR), BF),
            pltpu.SemaphoreType.DMA((2 + 3 * NX + 3 + NX + 1,)),
        ],
        cost_estimate=cost(100_000_000, 4_000_000, 200_000),
        compiler_params=WIDEST,
    )(sizes, q, k, v, extras, anc, *messages)


def late_kernel(w_hbm, m0, m1, m2, m3, w0_hbm, gates_hbm, w0, gates, sems):
    x, _ = place()
    pairs = [(m.at[pl.ds(0, NZ * NODES)], gates.at[n]) for n, m in enumerate((m0, m1, m2, m3))]
    pairs.append((w_hbm.at[:, pl.ds(pl.multiple_of(x * QUART, QUART), QUART)], w0))
    copies = run_copies(pairs, sems)
    sends = [pltpu.make_async_copy(gates.at[n], gates_hbm.at[n], sems.at[len(pairs) + n]) for n in range(NX)]
    sends.append(pltpu.make_async_copy(w0, w0_hbm, sems.at[len(pairs) + NX]))
    for copy, send in zip(copies, sends):
        copy.wait()
        send.start()
    for send in sends:
        send.wait()


def late_part(w, messages):
    return pl.pallas_call(
        late_kernel,
        in_specs=[HBM] * 5,
        out_specs=[HBM] * 2,
        out_shape=[jax.ShapeDtypeStruct((COLS, QUART), BF), jax.ShapeDtypeStruct((NX, NZ * NODES, PAIR), BF)],
        scratch_shapes=[
            pltpu.VMEM((COLS, QUART), BF),
            pltpu.VMEM((NX, NZ * NODES, PAIR), BF),
            pltpu.SemaphoreType.DMA((2 * NX + 2,)),
        ],
        cost_estimate=cost(0, 3_000_000),
        compiler_params=WIDEST,
    )(w, *messages)


def merge_kernel(sizes, inter_hbm, gain_hbm, extras_hbm, anc_hbm, *refs):
    intras, gates, refs = refs[:NX], refs[NX], refs[NX + 1 :]
    out, inter_ref, gate_ref, gain, extras, tree, square_ref, sems = refs
    x, z = place()
    spots = [lax.rem(x - slot + NX, NX) for slot in range(NX)]
    pairs = [(inter_hbm, inter_ref), (extras_hbm.at[pl.ds(x * NZ, NZ)], extras)]
    pairs.append((gain_hbm.at[pl.ds(pl.multiple_of(x * 2 * NZ, 2 * NZ), 2 * NZ)], gain))
    for slot, xa in enumerate(spots):
        pairs.append((anc_hbm.at[xa * NZ + z], tree.at[slot]))
        pairs.append((gates.at[slot], gate_ref.at[slot]))
    copies = run_copies(pairs, sems)
    node = lax.broadcasted_iota(jnp.int32, (NODES, HD), 0)
    lane = lax.broadcasted_iota(jnp.int32, (1, HD), 1)
    copies[1].wait()
    rates = jnp.zeros((1, HD), F32)
    for h in range(2 * NZ):
        rates = jnp.where(lane == h, decay_rows(extras[h // 2])[h % 2], rates)
    copies[0].wait()
    copies[2].wait()
    for slot, xa in enumerate(spots):
        rows = pl.ds(pl.multiple_of(xa * NODES, NODES), NODES)
        half = lax.div(xa, 2)
        near = lax.rem(xa, 2) * NODES
        for copy in copies[3 + 2 * slot : 5 + 2 * slot]:
            copy.wait()
        depth = jnp.sum(tree[slot].astype(F32), axis=1, keepdims=True)
        live = (node < sizes[xa * NZ + z]).astype(F32)
        fade = live * jnp.exp(-rates * depth)
        squares = jnp.zeros((NODES, HD), F32)
        for h in range(2 * NZ):
            lanes = slice((h % 2) * HD, (h % 2 + 1) * HD)
            inter = inter_ref[h // 2, rows, lanes].astype(F32)
            intra = intras[slot][:, h * HD : (h + 1) * HD].astype(F32)
            attn = (fade[:, h : h + 1] * inter + intra).astype(BF).astype(F32)
            squares = squares + attn * attn
            gate = gate_ref[slot, (h // 2) * NODES : (h // 2 + 1) * NODES, lanes].astype(F32)
            place_rows = pl.ds(pl.multiple_of(h * HROWS + near, NODES), NODES)
            out[half, place_rows, :] = (attn * gain[h : h + 1, :] / (1.0 + jnp.exp(-gate))).astype(BF)
        square_ref[rows, :] = squares
    ones = jnp.ones((16, HD), BF)
    total = jnp.zeros((16, ROWS), F32)
    for piece in split3(square_ref[...]):
        total = total + lax.dot_general(ones, piece.astype(BF), NT, preferred_element_type=F32)
    row = lax.broadcasted_iota(jnp.int32, (16, ROWS), 0)
    hi, mid, low = split3(total)
    tail = jnp.where(row == 0, hi, jnp.where(row == 1, mid, jnp.where(row == 2, low, 0.0))).astype(BF)
    for half in range(2):
        out[half, 16 * HROWS :, :] = tail


def merge(sizes, inter, gain, extras, anc, intras, gates):
    return pl.pallas_call(
        merge_kernel,
        in_specs=[SMEM] + [HBM] * 4 + [VMEM] * NX + [HBM],
        out_specs=VMEM,
        out_shape=jax.ShapeDtypeStruct((2, PIECE, HD), BF),
        scratch_shapes=[
            pltpu.VMEM((NZ, ROWS, PAIR), BF),
            pltpu.VMEM((NX, NZ * NODES, PAIR), BF),
            pltpu.VMEM((2 * NZ, HD), F32),
            pltpu.VMEM((NZ, EXTRA, HD), BF),
            pltpu.VMEM((NX, NODES, NODES), jnp.int32),
            pltpu.VMEM((ROWS, HD), F32),
            pltpu.SemaphoreType.DMA((3 + 2 * NX,)),
        ],
        cost_estimate=cost(10_000_000, 4_000_000),
        compiler_params=PARAMS,
    )(sizes, inter, gain, extras, anc, *intras, gates)


def project_kernel(count, *refs):
    pieces, weights, outs, u = refs[:count], refs[count], refs[count + 1 : count + 1 + NX], refs[-1]
    if len(pieces[0].shape) == 3:
        halves = [piece.at[half] for piece in pieces for half in range(2)]
        tails = [piece[0, 16 * HROWS :, :] for piece in pieces]
    else:
        halves = pieces
        lane = lax.broadcasted_iota(jnp.int32, (16, ROWS), 1)
        first, second = (piece[16 * HROWS :, :].astype(F32) for piece in pieces)
        tails = [jnp.where(lane < HROWS, first, second).astype(BF)]
    for n, half in enumerate(halves):
        for h in range(2 * NZ):
            u[n * HROWS : (n + 1) * HROWS, h * HD : (h + 1) * HD] = half[h * HROWS : (h + 1) * HROWS, :]
    acc = lax.dot_general(weights[...], u[...], NT, preferred_element_type=F32)
    for n, out in enumerate(outs):
        out[:COLS, :] = acc[n * COLS : (n + 1) * COLS].astype(out.dtype)
        for p, tail in enumerate(tails):
            out[COLS:, p * ROWS : (p + 1) * ROWS] = tail.astype(out.dtype)


def project(pieces, weights):
    rows = ROWS * len(pieces) if pieces[0].ndim == 3 else ROWS
    shape = (COLS + 16, rows)
    return pl.pallas_call(
        functools.partial(project_kernel, len(pieces)),
        in_specs=[VMEM] * (len(pieces) + 1),
        out_specs=[VMEM] * NX,
        out_shape=[jax.ShapeDtypeStruct(shape, F32)] + [jax.ShapeDtypeStruct(shape, BF)] * (NX - 1),
        scratch_shapes=[pltpu.VMEM((rows, QUART), BF)],
        cost_estimate=cost(2 * rows * QUART * COLS * NX, 4_000_000),
        compiler_params=PARAMS,
    )(*pieces, weights)


def finish_kernel(layout, *refs):
    out_hbm, out, sems = refs[-3:]
    _, z = place()
    sends = []
    for g, shifts in enumerate(layout):
        parts = refs[4 * g : 4 * g + 4]
        for p, shift in enumerate(shifts):
            cols = slice(p * ROWS, (p + 1) * ROWS)
            total = sum(part[:, cols].astype(F32) for part in parts)
            squares = total[COLS : COLS + 1] + total[COLS + 1 : COLS + 2] + total[COLS + 2 : COLS + 3]
            scaled = total[:COLS] * lax.rsqrt(squares * (1.0 / (HEADS * HD)) + 1e-06)
            rest = jnp.concatenate([scaled[HD:], jnp.zeros((2 * HD - COLS, ROWS), F32)])
            left, right = scaled[:HD].T, rest.T
            source = lax.rem(z - shift + 2 * NZ, NZ)
            for x in range(NX):
                n = len(sends)
                rows = slice(x * NODES, (x + 1) * NODES)
                out[n, :, :HD] = left[rows].astype(BF)
                out[n, :, HD:] = right[rows, : COLS - HD].astype(BF)
                sends.append(pltpu.make_async_copy(out.at[n], out_hbm.at[x, source], sems.at[n]))
                sends[-1].start()
    for send in sends:
        send.wait()


def finish(groups, layout, before=None):
    flat = [a for group in groups for a in group]
    blocks = NX * sum(len(shifts) for shifts in layout)
    extra = [] if before is None else [before]
    return pl.pallas_call(
        functools.partial(finish_kernel, layout),
        in_specs=[VMEM] * len(flat) + [HBM] * len(extra),
        out_specs=HBM,
        out_shape=jax.ShapeDtypeStruct((NX, NZ, NODES, COLS), BF),
        scratch_shapes=[pltpu.VMEM((blocks, NODES, COLS), BF), pltpu.SemaphoreType.DMA((blocks,))],
        input_output_aliases={len(flat): 0} if extra else {},
        cost_estimate=cost(2_000_000, 4_000_000),
        compiler_params=PARAMS,
    )(*flat, *extra)


ZLINES = [[x * NZ + z for z in range(NZ)] for x in range(NX)]


def tie(arrays, *marks):
    return lax.optimization_barrier((*arrays, *marks))[: len(arrays)]


def per_device(queries, keys, values, gate, states, decay, ancestors, tree_sizes, gain, out_weight):
    packed = pack_queries(decay, queries)
    m0, m1, m2, m3 = pack_messages(gate, out_weight.T, packed)
    m2, m1, m3 = xsend(m2, 2), xsend(m1, 1), xsend(m3, 3)
    spread = lax.all_to_all(packed, "head", 0, 0, tiled=True)
    inter, extras = inter_part(spread, states, [])
    (inter,) = tie((inter,), m1, m3)
    inter = lax.all_to_all(inter, "head", 0, 0, axis_index_groups=ZLINES, tiled=True)
    t0, t1, t2, t3, mine = intra_part(tree_sizes, queries, keys, values, extras, ancestors, (m1, m2, m3))
    t2, t1, t3 = xsend(t2, 2), xsend(t1, 1), xsend(t3, 3)
    w0, gates = late_part(out_weight.T, tie((m0, m1, m2, m3), t1))
    yours = swap_y(mine)
    gain = gain.reshape(HEADS, HD)
    own = merge(tree_sizes, inter, gain, extras, ancestors, (t0, t1, t2, t3), gates)
    theirs = swap_core(jnp.stack(tie((mine, yours), own)))
    weights = join_weights(w0, mine, yours, theirs)

    groups, layout = [], []

    def send_sums(pieces, places):
        own_part, *others = project(pieces, weights)
        groups.append([own_part] + [xsend(p, -d) for d, p in enumerate(others, 1)])
        layout.append(places)
        return own_part

    up, dn = zsend(own, 1), zsend(own, -1)
    mark = send_sums([own], [0])
    for step in range(1, 4):
        up, dn = tie((up, dn), *groups[-1])
        pieces = up, dn
        if step < 3:
            up, dn = zsend(up, 1), zsend(dn, -1)
        else:
            up, dn = zsend(up[0], 1), zsend(dn[1], -1)
        mark = send_sums(pieces, [step, -step])
    last = tie((up, dn), mark)
    send_sums(last, [4])
    out = finish(groups[:3], layout[:3])
    out = finish(groups[3:], layout[3:], out)
    return out.reshape(NX * NZ, NODES, COLS)


def solution(mesh):
    return jax.shard_map(
        per_device,
        mesh=mesh,
        in_specs=(
            P(("dp", "head"), None, None),
            P(("dp", "head"), None, None),
            P(("dp", "head"), None, None),
            P(("dp", "head"), None, None),
            P("dp", "head", None, None),
            P("head"),
            P("dp", None, None),
            P("dp"),
            P(),
            P(None, "head"),
        ),
        out_specs=P("dp", None, "head"),
        check_vma=False,
    )
```

```python
import functools
import jax
import jax.numpy as jnp
from jax import lax
from jax.experimental import pallas as pl
from jax.experimental.pallas import tpu as pltpu
from jax.sharding import PartitionSpec as P

NX = 4
NZ = 8
NODES = 32
HEADS = 64
HD = 128
PAIR = 2 * HD
QUART = 2048
PART = QUART // 4

NY = 4
COLS = 192
MSG = NODES * 8 + 2 * COLS
HROWS = 64
PIECE = 16 * HROWS + 16
ROWS = NX * NODES
EXTRA = 8
QROWS = 2 * NODES + EXTRA
NT = (((1,), (1,)), ((), ()))
BF = jnp.bfloat16
F32 = jnp.float32
ANY = pl.BlockSpec(memory_space=pl.ANY)
HBM = pl.BlockSpec(memory_space=pltpu.HBM)
VMEM = pl.BlockSpec(memory_space=pltpu.VMEM)
SMEM = pl.BlockSpec(memory_space=pltpu.SMEM)
WIDEST = pltpu.CompilerParams(vmem_limit_bytes=60 * 1024 * 1024)
PARAMS = pltpu.CompilerParams(vmem_limit_bytes=16 * 1024 * 1024)


def zsend(array, shift):
    pairs = [(x * NZ + z, x * NZ + (z + shift) % NZ) for x in range(NX) for z in range(NZ)]
    return lax.ppermute(array, "head", pairs)


def xsend(array, shift):
    pairs = [(x * NZ + z, ((x + shift) % NX) * NZ + z) for x in range(NX) for z in range(NZ)]
    return lax.ppermute(array, "head", pairs)


def swap_y(array):
    return lax.ppermute(array, "dp", [(i, i ^ 2) for i in range(2 * NY)])


def swap_core(array):
    return lax.ppermute(array, "dp", [(i, i ^ 1) for i in range(2 * NY)])


def place():
    me = lax.axis_index("head")
    return lax.div(me, NZ), lax.rem(me, NZ)


def cost(flops, size, trans=0):
    return pl.CostEstimate(flops=flops, bytes_accessed=size, transcendentals=trans)


def run_copies(pairs, sems):
    copies = [pltpu.make_async_copy(a, b, sems.at[n]) for n, (a, b) in enumerate(pairs)]
    for copy in copies:
        copy.start()
    return copies


def split3(value):
    hi = value.astype(BF).astype(F32)
    mid = (value - hi).astype(BF).astype(F32)
    return hi, mid, value - hi - mid


def pack_queries_kernel(decay, q_hbm, out_hbm, out, q, sems):
    cuts = [slice(n * QUART, (n + 1) * QUART) for n in range(NX)]
    copies = run_copies([(q_hbm.at[0, :, cut], q.at[:, cut]) for cut in cuts], sems)
    row = lax.broadcasted_iota(jnp.int32, (EXTRA, HD), 0)
    rows = jnp.zeros((EXTRA, HD), F32)
    for j in range(2):
        for n, piece in enumerate(split3(jnp.full((EXTRA, HD), decay[j], F32))):
            rows = jnp.where(row == 3 * j + n, piece, rows)
    tail = rows.astype(BF)
    for n in range(NX * NZ):
        out[n, 2 * NODES :, :] = tail
    sends = []
    for x in range(NX):
        copies[x].wait()
        for n in range(x * NZ, (x + 1) * NZ):
            for j in range(2):
                out[n, j * NODES : (j + 1) * NODES, :] = q[:, (2 * n + j) * HD : (2 * n + j + 1) * HD]
        cut = pl.ds(x * NZ, NZ)
        sends.append(pltpu.make_async_copy(out.at[cut], out_hbm.at[cut], sems.at[NX + x]))
        sends[-1].start()
    for send in sends:
        send.wait()


def pack_queries(decay, q):
    return pl.pallas_call(
        pack_queries_kernel,
        in_specs=[SMEM, HBM],
        out_specs=HBM,
        out_shape=jax.ShapeDtypeStruct((NX * NZ, QROWS, HD), BF),
        scratch_shapes=[
            pltpu.VMEM((NX * NZ, QROWS, HD), BF),
            pltpu.VMEM((NODES, HEADS * HD), BF),
            pltpu.SemaphoreType.DMA((2 * NX,)),
        ],
        cost_estimate=cost(0, 1_000_000),
        compiler_params=WIDEST,
    )(decay, q)


def pack_messages_kernel(gate_hbm, w, after, *refs):
    outs_hbm, (gate, outs, sems) = refs[:NX], refs[NX:]
    x, _ = place()
    cuts = [slice(n * QUART, (n + 1) * QUART) for n in range(NX)]
    pairs = [(gate_hbm.at[0, :, cut], gate.at[:, cut]) for cut in cuts]
    bases = [lax.rem(x + n, NX) * QUART for n in range(NX)]
    for n in (2, 1, 3):
        for b in range(2):
            col = pl.multiple_of(bases[n] + lax.rem(lax.axis_index("dp"), 4) * PART + b * PAIR, PAIR)
            pairs.append((w.at[:, pl.ds(col, PAIR)], outs.at[n, pl.ds(NZ * NODES + b * COLS, COLS)]))
    copies = run_copies(pairs, sems)
    for copy in copies[:NX]:
        copy.wait()
    sends = []
    for i, n in enumerate((2, 1, 3, 0)):
        for b in range(NZ):
            cols = pl.ds(pl.multiple_of(bases[n] + b * PAIR, PAIR), PAIR)
            outs[n, b * NODES : (b + 1) * NODES, :] = gate[:, cols]
        rows = pl.ds(0, NZ * NODES)
        if n:
            copies[NX + 2 * i].wait()
            copies[NX + 2 * i + 1].wait()
            rows = pl.ds(0, MSG)
        sends.append(pltpu.make_async_copy(outs.at[n, rows], outs_hbm[n].at[rows], sems.at[len(pairs) + n]))
        sends[-1].start()
    for send in sends:
        send.wait()


def pack_messages(gate, w, after):
    return pl.pallas_call(
        pack_messages_kernel,
        in_specs=[HBM] * 2 + [ANY],
        out_specs=[HBM] * NX,
        out_shape=[jax.ShapeDtypeStruct((NZ * NODES, PAIR), BF)]
        + [jax.ShapeDtypeStruct((MSG, PAIR), BF)] * (NX - 1),
        scratch_shapes=[
            pltpu.VMEM((NODES, HEADS * HD), BF),
            pltpu.VMEM((NX, MSG, PAIR), BF),
            pltpu.SemaphoreType.DMA((NX + 6 + NX,)),
        ],
        cost_estimate=cost(0, 4_000_000),
        compiler_params=WIDEST,
    )(gate, w, after)


def join_weights_kernel(w0, m0, m1, theirs, out):
    part = lax.rem(lax.axis_index("dp"), 4)
    flip = 1 - 2 * lax.rem(part, 2)
    far = lax.rem(part + 2, 4)
    out[:COLS, :] = w0[...]
    for s, (ref, mine) in enumerate(((m0, part), (m1, far))):
        for d in range(NX - 1):
            for b in range(2):
                near = pl.ds(pl.multiple_of(mine * PART + b * PAIR, PAIR), PAIR)
                other = pl.ds(pl.multiple_of((mine + flip) * PART + b * PAIR, PAIR), PAIR)
                out[(d + 1) * COLS : (d + 2) * COLS, near] = ref[d, b * COLS : (b + 1) * COLS]
                out[(d + 1) * COLS : (d + 2) * COLS, other] = theirs[s, d, b * COLS : (b + 1) * COLS]


def join_weights(w0, m0, m1, theirs):
    return pl.pallas_call(
        join_weights_kernel,
        in_specs=[VMEM] * 4,
        out_specs=VMEM,
        out_shape=jax.ShapeDtypeStruct((NX * COLS, QUART), BF),
        cost_estimate=cost(0, 6_000_000),
        compiler_params=PARAMS,
    )(w0, m0, m1, theirs)


def inter_kernel(queries, states, out_hbm, extras_hbm, out, extras, sems):
    sends = []
    for z in range(NZ):
        for x in range(NX):
            r = x * NZ + z
            for j in range(2):
                rows = slice(j * NODES, (j + 1) * NODES)
                inter = jnp.dot(queries[r, rows, :], states[r, j], preferred_element_type=F32)
                out[z, x * NODES : (x + 1) * NODES, j * HD : (j + 1) * HD] = inter.astype(BF)
            extras[r] = queries[r, 2 * NODES :, :]
        sends.append(pltpu.make_async_copy(out.at[z], out_hbm.at[z], sems.at[z]))
        sends[-1].start()
    sends.append(pltpu.make_async_copy(extras, extras_hbm, sems.at[NZ]))
    sends[-1].start()
    for send in sends:
        send.wait()


def inter_part(queries, states):
    return pl.pallas_call(
        inter_kernel,
        in_specs=[VMEM] * 2,
        out_specs=[HBM] * 2,
        out_shape=[
            jax.ShapeDtypeStruct((NZ, ROWS, PAIR), BF),
            jax.ShapeDtypeStruct((NX * NZ, EXTRA, HD), BF),
        ],
        scratch_shapes=[
            pltpu.VMEM((NZ, ROWS, PAIR), BF),
            pltpu.VMEM((NX * NZ, EXTRA, HD), BF),
            pltpu.SemaphoreType.DMA((NZ + 1,)),
        ],
        cost_estimate=cost(70_000_000, 4_000_000, 100_000),
        compiler_params=PARAMS,
    )(queries, states)


def decay_rows(extra):
    extra = extra.astype(F32)
    return [extra[3 * j : 3 * j + 1] + extra[3 * j + 1 : 3 * j + 2] + extra[3 * j + 2 : 3 * j + 3] for j in range(2)]


def intra_kernel(sizes, q_hbm, k_hbm, v_hbm, extras_hbm, anc_hbm, m1, m2, m3, *refs):
    outs_hbm, (weights_hbm, parts, extras, tree, out, weights, sems) = refs[:NX], refs[NX:]
    me = lax.axis_index("head")
    x, _ = place()
    order = (2, 1, 3, 0)
    quarters = [lax.rem(x + n, NX) for n in order]
    pairs = [(anc_hbm.at[me], tree), (extras_hbm, extras)]
    for n, quarter in zip(order, quarters):
        cut = pl.ds(pl.multiple_of(quarter * QUART, QUART), QUART)
        pairs += [(ref.at[0, :, cut], parts.at[n, i]) for i, ref in enumerate((q_hbm, k_hbm, v_hbm))]
    pairs += [(m.at[pl.ds(NZ * NODES, 2 * COLS)], weights.at[n]) for n, m in enumerate((m1, m2, m3))]
    copies = run_copies(pairs, sems)
    node = lax.broadcasted_iota(jnp.int32, (NODES, HD), 0)
    lane = lax.broadcasted_iota(jnp.int32, (NODES, HD), 1)
    live = (node < sizes[me]).astype(F32)
    copies[0].wait()
    copies[1].wait()
    anc = tree[...].astype(F32)
    depth = jnp.sum(anc, axis=1, keepdims=True)
    depth_t = lax.dot_general(jnp.ones((8, NODES), BF), anc.astype(BF), NT, preferred_element_type=F32)[0:1]
    blocks = HD // NODES
    wide_anc = jnp.concatenate([anc] * blocks, axis=1)
    wide_gaps = jnp.concatenate([depth - depth_t] * blocks, axis=1)
    own = [lane // NODES == n for n in range(blocks)]
    mask = jnp.concatenate([jnp.where(m, wide_anc, 0.0) for m in own])
    gaps = jnp.concatenate([jnp.where(m, wide_gaps, 0.0) for m in own])
    sends = []
    for i, (shift, quarter) in enumerate(zip(order, quarters)):
        for n in range(3):
            copies[2 + 3 * i + n].wait()
        for first in range(0, 2 * NZ, blocks):
            heads = range(first, first + blocks)
            q, k, v = (jnp.concatenate([parts[shift, n, :, h * HD : (h + 1) * HD] for h in heads]) for n in range(3))
            rates = []
            for h in heads:
                rate = decay_rows(extras[quarter * NZ + h // 2])[h % 2]
                rates.append(jnp.broadcast_to(rate, (NODES, HD)))
            scores = lax.dot_general(q, k, NT, preferred_element_type=F32)
            mix = (scores * (mask * jnp.exp(-jnp.concatenate(rates) * gaps))).astype(BF)
            intra = jnp.dot(mix, v, preferred_element_type=F32)
            for n, h in enumerate(heads):
                out[shift, :, h * HD : (h + 1) * HD] = (live * intra[n * NODES : (n + 1) * NODES]).astype(BF)
        sends.append(pltpu.make_async_copy(out.at[shift], outs_hbm[shift], sems.at[len(pairs) + shift]))
        sends[-1].start()
        if i == 1:
            for copy in copies[2 + 3 * NX :]:
                copy.wait()
            sends.append(pltpu.make_async_copy(weights, weights_hbm, sems.at[len(pairs) + NX]))
            sends[-1].start()
    for send in sends:
        send.wait()


def intra_part(sizes, q, k, v, extras, anc, messages):
    return pl.pallas_call(
        intra_kernel,
        in_specs=[SMEM] + [HBM] * 8,
        out_specs=[HBM] * (NX + 1),
        out_shape=[jax.ShapeDtypeStruct((NODES, QUART), BF)] * NX
        + [jax.ShapeDtypeStruct((NX - 1, 2 * COLS, PAIR), BF)],
        scratch_shapes=[
            pltpu.VMEM((NX, 3, NODES, QUART), BF),
            pltpu.VMEM((NX * NZ, EXTRA, HD), BF),
            pltpu.VMEM((NODES, NODES), jnp.int32),
            pltpu.VMEM((NX, NODES, QUART), BF),
            pltpu.VMEM((NX - 1, 2 * COLS, PAIR), BF),
            pltpu.SemaphoreType.DMA((2 + 3 * NX + 3 + NX + 1,)),
        ],
        cost_estimate=cost(100_000_000, 4_000_000, 200_000),
        compiler_params=WIDEST,
    )(sizes, q, k, v, extras, anc, *messages)


def late_kernel(w_hbm, m0, m1, m2, m3, w0_hbm, gates_hbm, w0, gates, sems):
    x, _ = place()
    pairs = [(m.at[pl.ds(0, NZ * NODES)], gates.at[n]) for n, m in enumerate((m0, m1, m2, m3))]
    pairs.append((w_hbm.at[:, pl.ds(pl.multiple_of(x * QUART, QUART), QUART)], w0))
    copies = run_copies(pairs, sems)
    sends = [pltpu.make_async_copy(gates.at[n], gates_hbm.at[n], sems.at[len(pairs) + n]) for n in range(NX)]
    sends.append(pltpu.make_async_copy(w0, w0_hbm, sems.at[len(pairs) + NX]))
    for copy, send in zip(copies, sends):
        copy.wait()
        send.start()
    for send in sends:
        send.wait()


def late_part(w, messages):
    return pl.pallas_call(
        late_kernel,
        in_specs=[HBM] * 5,
        out_specs=[HBM] * 2,
        out_shape=[jax.ShapeDtypeStruct((COLS, QUART), BF), jax.ShapeDtypeStruct((NX, NZ * NODES, PAIR), BF)],
        scratch_shapes=[
            pltpu.VMEM((COLS, QUART), BF),
            pltpu.VMEM((NX, NZ * NODES, PAIR), BF),
            pltpu.SemaphoreType.DMA((2 * NX + 2,)),
        ],
        cost_estimate=cost(0, 3_000_000),
        compiler_params=WIDEST,
    )(w, *messages)


def merge_kernel(sizes, inter_ref, gain_hbm, extras_hbm, anc_hbm, *refs):
    intras, gate_ref, refs = refs[:NX], refs[NX], refs[NX + 1 :]
    out, gain, extras, tree, square_ref, sems = refs
    x, z = place()
    spots = [lax.rem(x - slot + NX, NX) for slot in range(NX)]
    pairs = [(extras_hbm.at[pl.ds(x * NZ, NZ)], extras)]
    pairs.append((gain_hbm.at[pl.ds(pl.multiple_of(x * 2 * NZ, 2 * NZ), 2 * NZ)], gain))
    for slot, xa in enumerate(spots):
        pairs.append((anc_hbm.at[xa * NZ + z], tree.at[slot]))
    copies = run_copies(pairs, sems)
    node = lax.broadcasted_iota(jnp.int32, (NODES, HD), 0)
    lane = lax.broadcasted_iota(jnp.int32, (1, HD), 1)
    copies[0].wait()
    rates = jnp.zeros((1, HD), F32)
    for h in range(2 * NZ):
        rates = jnp.where(lane == h, decay_rows(extras[h // 2])[h % 2], rates)
    copies[1].wait()
    for slot, xa in enumerate(spots):
        rows = pl.ds(pl.multiple_of(xa * NODES, NODES), NODES)
        half = lax.div(xa, 2)
        near = lax.rem(xa, 2) * NODES
        copies[2 + slot].wait()
        depth = jnp.sum(tree[slot].astype(F32), axis=1, keepdims=True)
        live = (node < sizes[xa * NZ + z]).astype(F32)
        fade = live * jnp.exp(-rates * depth)
        squares = jnp.zeros((NODES, HD), F32)
        for h in range(2 * NZ):
            lanes = slice((h % 2) * HD, (h % 2 + 1) * HD)
            inter = inter_ref[h // 2, rows, lanes].astype(F32)
            intra = intras[slot][:, h * HD : (h + 1) * HD].astype(F32)
            attn = (fade[:, h : h + 1] * inter + intra).astype(BF).astype(F32)
            squares = squares + attn * attn
            gate = gate_ref[slot, (h // 2) * NODES : (h // 2 + 1) * NODES, lanes].astype(F32)
            place_rows = pl.ds(pl.multiple_of(h * HROWS + near, NODES), NODES)
            out[half, place_rows, :] = (attn * gain[h : h + 1, :] / (1.0 + jnp.exp(-gate))).astype(BF)
        square_ref[rows, :] = squares
    ones = jnp.ones((16, HD), BF)
    total = jnp.zeros((16, ROWS), F32)
    for piece in split3(square_ref[...]):
        total = total + lax.dot_general(ones, piece.astype(BF), NT, preferred_element_type=F32)
    row = lax.broadcasted_iota(jnp.int32, (16, ROWS), 0)
    hi, mid, low = split3(total)
    tail = jnp.where(row == 0, hi, jnp.where(row == 1, mid, jnp.where(row == 2, low, 0.0))).astype(BF)
    for half in range(2):
        out[half, 16 * HROWS :, :] = tail


def merge(sizes, inter, gain, extras, anc, intras, gates):
    return pl.pallas_call(
        merge_kernel,
        in_specs=[SMEM, VMEM] + [HBM] * 3 + [VMEM] * (NX + 1),
        out_specs=VMEM,
        out_shape=jax.ShapeDtypeStruct((2, PIECE, HD), BF),
        scratch_shapes=[
            pltpu.VMEM((2 * NZ, HD), F32),
            pltpu.VMEM((NZ, EXTRA, HD), BF),
            pltpu.VMEM((NX, NODES, NODES), jnp.int32),
            pltpu.VMEM((ROWS, HD), F32),
            pltpu.SemaphoreType.DMA((2 + NX,)),
        ],
        cost_estimate=cost(10_000_000, 4_000_000),
        compiler_params=PARAMS,
    )(sizes, inter, gain, extras, anc, *intras, gates)


def project_kernel(count, *refs):
    pieces, weights, outs, u = refs[:count], refs[count], refs[count + 1 : count + 1 + NX], refs[-1]
    if len(pieces[0].shape) == 3:
        halves = [piece.at[half] for piece in pieces for half in range(2)]
        tails = [piece[0, 16 * HROWS :, :] for piece in pieces]
    else:
        halves = pieces
        lane = lax.broadcasted_iota(jnp.int32, (16, ROWS), 1)
        first, second = (piece[16 * HROWS :, :].astype(F32) for piece in pieces)
        tails = [jnp.where(lane < HROWS, first, second).astype(BF)]
    for n, half in enumerate(halves):
        for h in range(2 * NZ):
            u[n * HROWS : (n + 1) * HROWS, h * HD : (h + 1) * HD] = half[h * HROWS : (h + 1) * HROWS, :]
    acc = lax.dot_general(weights[...], u[...], NT, preferred_element_type=F32)
    for n, out in enumerate(outs):
        out[:COLS, :] = acc[n * COLS : (n + 1) * COLS].astype(out.dtype)
        for p, tail in enumerate(tails):
            out[COLS:, p * ROWS : (p + 1) * ROWS] = tail.astype(out.dtype)


def project(pieces, weights):
    rows = ROWS * len(pieces) if pieces[0].ndim == 3 else ROWS
    shape = (COLS + 16, rows)
    return pl.pallas_call(
        functools.partial(project_kernel, len(pieces)),
        in_specs=[VMEM] * (len(pieces) + 1),
        out_specs=[VMEM] * NX,
        out_shape=[jax.ShapeDtypeStruct(shape, F32)] + [jax.ShapeDtypeStruct(shape, BF)] * (NX - 1),
        scratch_shapes=[pltpu.VMEM((rows, QUART), BF)],
        cost_estimate=cost(2 * rows * QUART * COLS * NX, 4_000_000),
        compiler_params=PARAMS,
    )(*pieces, weights)


def finish_kernel(layout, *refs):
    out_hbm, out, sems = refs[-3:]
    _, z = place()
    sends = []
    for g, shifts in enumerate(layout):
        parts = refs[4 * g : 4 * g + 4]
        for p, shift in enumerate(shifts):
            cols = slice(p * ROWS, (p + 1) * ROWS)
            total = sum(part[:, cols].astype(F32) for part in parts)
            squares = total[COLS : COLS + 1] + total[COLS + 1 : COLS + 2] + total[COLS + 2 : COLS + 3]
            scaled = total[:COLS] * lax.rsqrt(squares * (1.0 / (HEADS * HD)) + 1e-06)
            rest = jnp.concatenate([scaled[HD:], jnp.zeros((2 * HD - COLS, ROWS), F32)])
            left, right = scaled[:HD].T, rest.T
            source = lax.rem(z - shift + 2 * NZ, NZ)
            for x in range(NX):
                n = len(sends)
                rows = slice(x * NODES, (x + 1) * NODES)
                out[n, :, :HD] = left[rows].astype(BF)
                out[n, :, HD:] = right[rows, : COLS - HD].astype(BF)
                sends.append(pltpu.make_async_copy(out.at[n], out_hbm.at[x, source], sems.at[n]))
                sends[-1].start()
    for send in sends:
        send.wait()


def finish(groups, layout, before=None):
    flat = [a for group in groups for a in group]
    blocks = NX * sum(len(shifts) for shifts in layout)
    extra = [] if before is None else [before]
    return pl.pallas_call(
        functools.partial(finish_kernel, layout),
        in_specs=[VMEM] * len(flat) + [HBM] * len(extra),
        out_specs=HBM,
        out_shape=jax.ShapeDtypeStruct((NX, NZ, NODES, COLS), BF),
        scratch_shapes=[pltpu.VMEM((blocks, NODES, COLS), BF), pltpu.SemaphoreType.DMA((blocks,))],
        input_output_aliases={len(flat): 0} if extra else {},
        cost_estimate=cost(2_000_000, 4_000_000),
        compiler_params=PARAMS,
    )(*flat, *extra)


ZLINES = [[x * NZ + z for z in range(NZ)] for x in range(NX)]


def tie(arrays, *marks):
    return lax.optimization_barrier((*arrays, *marks))[: len(arrays)]


def per_device(queries, keys, values, gate, states, decay, ancestors, tree_sizes, gain, out_weight):
    packed = pack_queries(decay, queries)
    m0, m1, m2, m3 = pack_messages(gate, out_weight.T, packed)
    m2, m1, m3 = xsend(m2, 2), xsend(m1, 1), xsend(m3, 3)
    spread = lax.all_to_all(packed, "head", 0, 0, tiled=True)
    inter, extras = inter_part(spread, states)
    (inter,) = tie((inter,), m1, m3)
    inter = lax.all_to_all(inter, "head", 0, 0, axis_index_groups=ZLINES, tiled=True)
    t0, t1, t2, t3, mine = intra_part(tree_sizes, queries, keys, values, extras, ancestors, (m1, m2, m3))
    t2, t1, t3 = xsend(t2, 2), xsend(t1, 1), xsend(t3, 3)
    w0, gates = late_part(out_weight.T, tie((m0, m1, m2, m3), t1))
    yours = swap_y(mine)
    gain = gain.reshape(HEADS, HD)
    own = merge(tree_sizes, inter, gain, extras, ancestors, (t0, t1, t2, t3), gates)
    theirs = swap_core(jnp.stack(tie((mine, yours), own)))
    weights = join_weights(w0, mine, yours, theirs)

    groups, layout = [], []

    def send_sums(pieces, places):
        own_part, *others = project(pieces, weights)
        groups.append([own_part] + [xsend(p, -d) for d, p in enumerate(others, 1)])
        layout.append(places)
        return own_part

    up, dn = zsend(own, 1), zsend(own, -1)
    mark = send_sums([own], [0])
    for step in range(1, 4):
        up, dn = tie((up, dn), *groups[-1])
        pieces = up, dn
        if step < 3:
            up, dn = zsend(up, 1), zsend(dn, -1)
        else:
            up, dn = zsend(up[0], 1), zsend(dn[1], -1)
        mark = send_sums(pieces, [step, -step])
    last = tie((up, dn), mark)
    send_sums(last, [4])
    out = finish(groups[:3], layout[:3])
    out = finish(groups[3:], layout[3:], out)
    return out.reshape(NX * NZ, NODES, COLS)


def solution(mesh):
    return jax.shard_map(
        per_device,
        mesh=mesh,
        in_specs=(
            P(("dp", "head"), None, None),
            P(("dp", "head"), None, None),
            P(("dp", "head"), None, None),
            P(("dp", "head"), None, None),
            P("dp", "head", None, None),
            P("head"),
            P("dp", None, None),
            P("dp"),
            P(),
            P(None, "head"),
        ),
        out_specs=P("dp", None, "head"),
        check_vma=False,
    )
```
